512 devices in a mesh: var: 16 (over y_lo, z), patch: 8 (over x, core), dp: 4 (over y_hi).
Axes of the slice: x: 4, y: 8 (y_hi: 4, y_lo: 2; y = y_hi * 2 + y_lo), z: 8, core: 2. Of those that a mesh axis runs over, the one named last changes fastest.
Arguments:
- pixels: bfloat16 [64, 32, 64, 128], P('dp', 'var', None, 'patch'), may hold values from -6 to 6
- emb_weight: bfloat16 [32, 65536], P('var', ('patch', 'dp')), may hold values from -0.75 to 0.75
- chan_bias: bfloat16 [32, 1024], P('var')
- score_vecs: bfloat16 [1024, 16], replicated
- value_weight: bfloat16 [1024, 1024], replicated, may hold values from -0.1875 to 0.1875
- out_grad: bfloat16 [64, 128, 1024], P('dp', ('patch', 'var')), may hold values from -6 to 6
- slot_order: int32 [32], replicated, may hold values from 0 to 31, each once
Outputs:
- emb_weight_grad: float32 [32, 65536], P('var', ('patch', 'dp'))
- bias_grad: float32 [32, 1024], P('var', ('patch', 'dp'))
- score_grad: float32 [1024, 16], replicated
The draws below stay inside these ranges and needn't reach their ends.
Inputs may be any that keep to these rules, and one draw needn't show every extreme that they name: `slot_order`: each slot number appears once; slots holding 28 or more are padding.
All inputs are finite; a program needn't handle non-finite values.
Results may differ from the reference program's by a relative error of at most 0.012.
The reference program's roundings to bfloat16 on the way (of `tokens`, `proj`, `dscore_b` and `token_grad`) count: a program that leaves them out, or rounds other values in their place, can miss the bound.
Values may be sent and summed in bfloat16 or wider, within the bound.
A program may use at most 128 MiB of HBM per device.

```python
import jax
import jax.numpy as jnp
from jax import lax

D = 1024
HEADS = 16
PP = 64
PATCH_DEV = 16
C_PAD = 32
CHANNELS = 28
NP = 128
BATCH = 64


def shared_dirs(key):
    return jax.random.normal(key, (D, HEADS), jnp.float32)


def draw_score_vecs(key, part):
    base = shared_dirs(key)
    return (base * D ** (-0.5)).astype(jnp.bfloat16)


def draw_chan_bias(key, part):
    key = jax.random.fold_in(key, 12)
    noise = jax.random.normal(key, (C_PAD, D), jnp.float32) * 0.5
    return noise.astype(jnp.bfloat16)


def block_levels(stream_key, dims, shards, low, high):
    factor_of = 1.0
    for position, parts in shards:
        draws = jax.random.uniform(jax.random.fold_in(jax.random.fold_in(stream_key, 6), position), (parts,), jnp.float32, low / len(shards), high / len(shards))
        factor_of = factor_of * jnp.repeat(jnp.exp(draws), dims[position] // parts).reshape((-1,) + (1,) * (len(dims) - 1 - position))
    return factor_of


def gaussian(stream_key, extent, scale, limit, split=(), kind=jnp.bfloat16):
    level = block_levels(stream_key, extent, split, -0.22, 0.18) if split else 1.0
    entries = jax.random.normal(stream_key, extent, jnp.float32) * scale * level
    return jnp.minimum(jnp.maximum(entries, -limit), limit).astype(kind)


def setup_inputs(seed: int = 0) -> dict:
    splits = jax.random.split(jax.random.key(seed), 8)
    pixels = gaussian(splits[0], (BATCH, C_PAD, PP, NP), 1.0, 6.0, ((0, 4), (1, 16), (3, 8)))
    emb_weight = gaussian(splits[1], (C_PAD, PP * D), PP ** -0.5, 0.75, ((0, 16), (1, 32)))
    chan_bias = draw_chan_bias(jax.random.fold_in(splits[7], 71), 0)
    score_vecs = draw_score_vecs(jax.random.fold_in(splits[7], 71), 0)
    value_weight = gaussian(splits[4], (D, D), D ** -0.5, 0.1875)
    out_grad = gaussian(splits[5], (BATCH, NP, D), 1.0, 6.0, ((0, 4), (1, 128)))
    slot_order = jax.random.permutation(splits[6], C_PAD).astype(jnp.int32)
    return {"pixels": pixels, "emb_weight": emb_weight, "chan_bias": chan_bias, "score_vecs": score_vecs, "value_weight": value_weight, "out_grad": out_grad, "slot_order": slot_order}


def reference(pixels, emb_weight, chan_bias, score_vecs, value_weight, out_grad, slot_order):
    c_pad, width = chan_bias.shape
    heads = score_vecs.shape[1]
    head_dim = width // heads
    pix = pixels.shape[2]
    valid = slot_order < CHANNELS
    kernel = emb_weight.reshape(c_pad, pix, width).astype(jnp.float32)
    vecs = score_vecs.astype(jnp.float32)
    value_heads = value_weight.reshape(width, heads, head_dim).astype(jnp.float32)
    block = PATCH_DEV
    nblocks = NP // block

    def step(carry, index):
        wsum, bsum, usum = carry
        sample = (index // nblocks).astype(jnp.int32)
        start = ((index % nblocks) * block).astype(jnp.int32)
        whole = lax.dynamic_index_in_dim(pixels, sample, 0, keepdims=False)
        pix_blk = lax.dynamic_slice_in_dim(whole, start, block, 2).astype(jnp.float32)
        grads = lax.dynamic_index_in_dim(out_grad, sample, 0, keepdims=False)
        grad_blk = lax.dynamic_slice_in_dim(grads, start, block, 0).astype(jnp.float32)
        tokens = (jnp.einsum('ckn,ckd->cnd', pix_blk, kernel) + chan_bias.astype(jnp.float32)[:, None, :]).astype(jnp.bfloat16)
        tok32 = tokens.astype(jnp.float32)
        scores = jnp.einsum('cnd,dh->hcn', tok32, vecs)
        scores = jnp.where(valid[None, :, None], scores, jnp.float32(-1e30))
        peak = jnp.max(scores, axis=1)
        expo = jnp.exp(scores - peak[:, None, :])
        total = jnp.sum(expo, axis=1)
        proj = jnp.einsum('nhj,ihj->nhi', grad_blk.reshape(block, heads, head_dim), value_heads).astype(jnp.bfloat16)
        proj32 = proj.astype(jnp.float32)
        dprob = jnp.einsum('cnd,nhd->hcn', tok32, proj32)
        weighted = jnp.sum(expo * dprob, axis=1)
        probs = expo / total[:, None, :]
        dscore = probs * (dprob - (weighted / total)[:, None, :])
        probs_b = probs.astype(jnp.bfloat16).astype(jnp.float32)
        dscore_b = dscore.astype(jnp.bfloat16).astype(jnp.float32)
        token_grad = (jnp.einsum('hcn,nhd->cnd', probs_b, proj32) + jnp.einsum('hcn,dh->cnd', dscore_b, vecs)).astype(jnp.bfloat16)
        tg32 = token_grad.astype(jnp.float32)
        usum = usum + jnp.einsum('hcn,cnd->dh', dscore_b, tok32)
        wsum = wsum + jnp.einsum('ckn,cnd->ckd', pix_blk, tg32)
        bsum = bsum + jnp.sum(tg32, axis=1)
        return (wsum, bsum, usum), None

    init = (jnp.zeros((c_pad, pix, width), jnp.float32), jnp.zeros((c_pad, width), jnp.float32), jnp.zeros((width, heads), jnp.float32))
    (wsum, bsum, usum), unused = lax.scan(step, init, jnp.arange(BATCH * nblocks, dtype=jnp.int32))
    return wsum.reshape(c_pad, pix * width), bsum, usum
```

```python
import functools

import jax
import jax.numpy as jnp
from jax import lax
from jax.experimental import pallas as pl
from jax.experimental.pallas import tpu as pltpu
from jax.sharding import PartitionSpec as P

MESH = pl.DeviceIdType.MESH
F32 = jnp.float32
BF16 = jnp.bfloat16
CHUNK = 512
VCHUNK = 256


def mm(a, b, ca=1, cb=0):
    return lax.dot_general(
        a, b, (((ca,), (cb,)), ((), ())), preferred_element_type=F32
    )


def iota(shape, dim):
    return lax.broadcasted_iota(jnp.int32, shape, dim)


def kernel(
    sizes,
    slot_ref,
    pix_ref,
    wblk_ref,
    bias_ref,
    vecs_ref,
    og_ref,
    value_hbm,
    dw_ref,
    db_ref,
    du_ref,
    wv,
    mt,
    wbuf,
    wf,
    obuf,
    tok,
    uv,
    seg,
    spread,
    ut,
    zx,
    act,
    st_send,
    st_recv,
    res,
    stat,
    su_send,
    su_recv,
    sv_send,
    sv_recv,
    sw_recv,
    g_send,
    g_recv,
    gb_send,
    gb_recv,
    h_send,
    h_recv,
    hb_send,
    hb_recv,
    sem_wv,
    send,
    recv,
):
    nv, npa, nd, channels = sizes
    npd = npa * nd
    heads = nv
    v = lax.axis_index("var")
    p = lax.axis_index("patch")
    d = lax.axis_index("dp")
    pd = p * nd + d

    copy_wv = pltpu.make_async_copy(value_hbm, wv, sem_wv)
    copy_wv.start()

    def dev_v(q):
        return {"var": q}

    def dev_pd(q):
        return {"patch": q // nd, "dp": lax.rem(q, nd)}

    def dev_p(q):
        return {"patch": q}

    def dev_d(q):
        return {"dp": q}

    barrier = pltpu.get_barrier_semaphore()

    def greet(count, me, dev):
        def one(j, carry):
            pl.semaphore_signal(
                barrier,
                inc=1,
                device_id=dev(lax.rem(me + j, count)),
                device_id_type=MESH,
            )
            return carry

        lax.fori_loop(1, count, one, 0)

    greet(npd, pd, dev_pd)
    greet(nv, v, dev_v)

    def spray(k, count, me, dev, src, dst):
        def one(j, carry):
            q = lax.rem(me + j, count)
            pltpu.make_async_remote_copy(
                src_ref=src(q),
                dst_ref=dst.at[me],
                send_sem=send.at[k],
                recv_sem=recv.at[k],
                device_id=dev(q),
                device_id_type=MESH,
            ).start()
            return carry

        lax.fori_loop(1, count, one, 0)

    def gather_wait(sems, k, count, dst):
        part = dst.at[pl.ds(0, count - 1)]
        pltpu.make_async_copy(part, part, sems.at[k]).wait()

    pixf = pix_ref[...].astype(F32)
    rows, cols = pixf.shape
    odd = lax.rem(iota((rows, cols), 0), 2)
    mt[0:rows, 0:cols] = jnp.where(odd == 0, pixf, 0.0).astype(BF16)
    mt[0:rows, cols : 2 * cols] = jnp.where(odd == 1, pixf, 0.0).astype(BF16)
    tail = mt.shape[0] - rows
    ones = iota((tail, 2 * cols), 0) == iota((tail, 2 * cols), 1) // cols
    mt[rows:, :] = jnp.where(ones, 1.0, 0.0).astype(BF16)

    width = wv.shape[0]
    hd = width // heads
    uf = vecs_ref[...].astype(F32)
    uv[...] = jnp.zeros(uv.shape, BF16)
    uv[:, 0:heads] = uf.astype(BF16)
    head_of = iota((width, 128), 0) // hd
    lane = iota((width, 128), 1)
    seg[...] = jnp.where(lane == head_of + heads, 1.0, 0.0).astype(BF16)
    spread[...] = jnp.where(
        iota((128, width), 1) // hd == iota((128, width), 0), 1.0, 0.0
    ).astype(BF16)
    ut[...] = jnp.zeros(ut.shape, BF16)
    ut[heads : 2 * heads, :] = jnp.transpose(uv[...].astype(F32))[0:heads].astype(BF16)

    wf[rows:, :] = jnp.zeros((tail, width), F32)
    wf[rows : rows + 2, :] = bias_ref[...].astype(F32)
    wbuf[pd] = wblk_ref[...]
    obuf[v] = og_ref[...]

    pl.semaphore_wait(barrier, nv - 1 + npd - 1)

    spray(0, npd, pd, dev_pd, lambda q: wblk_ref, wbuf)
    spray(1, nv, v, dev_v, lambda q: og_ref, obuf)

    gather_wait(recv, 0, npd, wbuf)
    cw = wblk_ref.shape[1]
    for i in range(npd // 2):
        a = wbuf[2 * i].astype(F32)
        b = wbuf[2 * i + 1].astype(F32)
        for cc in range(4):
            wf[8 * i : 8 * i + 4, cw * cc : cw * (cc + 1)] = a[4 * cc : 4 * cc + 4]
            wf[8 * i + 4 : 8 * i + 8, cw * cc : cw * (cc + 1)] = b[4 * cc : 4 * cc + 4]
    for j in range(width // CHUNK):
        sl = slice(CHUNK * j, CHUNK * (j + 1))
        tok[:, sl] = mm(mt[...], wf[:, sl].astype(BF16), 0, 0).astype(BF16)

    zx[...] = mm(tok[...], uv[...])
    copy_wv.wait()
    gather_wait(recv, 1, nv, obuf)

    def products(j, carry):
        at = pl.multiple_of(j * VCHUNK, VCHUNK)
        vals = mm(tok[...], wv[:, pl.ds(at, VCHUNK)])
        grad = obuf[:, :, pl.ds(at, VCHUNK)].astype(F32).reshape(cols, VCHUNK)
        z = vals * jnp.concatenate([grad, grad], axis=0)
        hi = z.astype(BF16)
        lo = (z - hi.astype(F32)).astype(BF16)
        part = seg[pl.ds(at, VCHUNK), :]
        zx[...] += mm(hi, part) + mm(lo, part)
        return carry

    lax.fori_loop(0, width // VCHUNK, products, 0)
    xt = jnp.transpose(zx[...])
    sc, dp = [], []
    for c in range(2):
        s = xt[0:heads, cols * c : cols * (c + 1)]
        slot = jnp.full(s.shape, slot_ref[2 * v + c], jnp.int32)
        sc.append(jnp.where(slot < channels, s, -1e30))
        dp.append(xt[heads : 2 * heads, cols * c : cols * (c + 1)])

    top = jnp.maximum(sc[0], sc[1])
    e0, e1 = jnp.exp(sc[0] - top), jnp.exp(sc[1] - top)
    total = e0 + e1
    weighted = e0 * dp[0] + e1 * dp[1]
    for h in range(heads):
        for k, x in enumerate((top, total, weighted)):
            st_send[h, 2 * k : 2 * k + 1, :] = x[h : h + 1, 0:128]
            st_send[h, 2 * k + 1 : 2 * k + 2, :] = x[h : h + 1, 128:256]
    spray(2, nv, v, dev_v, lambda q: st_send.at[q], st_recv)
    st_recv[v] = st_send[v]
    gather_wait(recv, 2, nv, st_recv)
    got = st_recv[...]
    tops = got[:, 0:2, :]
    peak = jnp.max(tops, axis=0)
    scale = jnp.exp(tops - peak[None])
    total = jnp.sum(scale * got[:, 2:4, :], axis=0)
    ratio = jnp.sum(scale * got[:, 4:6, :], axis=0) / total
    res[v, 0:2, :] = peak
    res[v, 2:4, :] = total
    res[v, 4:6, :] = ratio
    spray(3, nv, v, dev_v, lambda q: res.at[v], res)
    gather_wait(recv, 3, nv, res)
    for h in range(heads):
        for k in range(3):
            stat[k, h : h + 1, 0:128] = res[h, 2 * k : 2 * k + 1, :]
            stat[k, h : h + 1, 128:256] = res[h, 2 * k + 1 : 2 * k + 2, :]
    peak, total, ratio = stat[0], stat[1], stat[2]
    probs = [jnp.exp(s - peak) / total for s in sc]
    dscore = [a * (b - ratio) for a, b in zip(probs, dp)]
    both = jnp.concatenate(
        [
            jnp.concatenate(probs, axis=1),
            jnp.concatenate(dscore, axis=1),
            jnp.zeros((128 - 2 * heads, 2 * cols), F32),
        ],
        axis=0,
    )

    part = mm(jnp.concatenate(dscore, axis=1).astype(BF16), tok[...])
    for h in range(heads):
        for k in range(width // 128):
            su_send[h, k : k + 1, :] = part[h : h + 1, 128 * k : 128 * (k + 1)]
    spray(4, nv, v, dev_v, lambda q: su_send.at[q], su_recv)
    su_recv[v] = su_send[v]

    q = jnp.transpose(both).astype(BF16)
    grad = obuf[...].reshape(cols, width)
    for j in range(width // CHUNK):
        sl = slice(CHUNK * j, CHUNK * (j + 1))
        g = grad[:, sl].astype(F32)
        act[:, sl] = (
            mm(q, spread[:, sl]) * jnp.concatenate([g, g], axis=0)
        ).astype(BF16)
    for j in range(width // CHUNK):
        sl = slice(CHUNK * j, CHUNK * (j + 1))
        tg = (mm(act[...], wv[sl, :], 1, 1) + mm(q, ut[:, sl])).astype(BF16)
        g = mm(mt[...], tg)
        for a in range(npa):
            g_send[j, a] = g[16 * a : 16 * (a + 1)]
        for a in range(CHUNK // 128):
            gb_send[j * (CHUNK // 128) + a, 0:2, :] = g[
                rows : rows + 2, 128 * a : 128 * (a + 1)
            ]
        spray(10 + j, npa, p, dev_p, lambda q, j=j: g_send.at[j, q], g_recv.at[j])
    spray(7, npa, p, dev_p, lambda q: gb_send.at[q], gb_recv)

    gather_wait(recv, 4, nv, su_recv)
    su = jnp.sum(su_recv[...], axis=0)
    sv_send[...] = su
    spray(5, npd, pd, dev_pd, lambda q: sv_send, sv_recv)
    sv_recv[pd] = su

    for j in range(width // CHUNK):
        g_recv[j, p] = g_send[j, p]
        gather_wait(recv, 10 + j, npa, g_recv.at[j])
        g = jnp.sum(g_recv[j].astype(F32), axis=0)
        for a in range(nd):
            h_send[a, :, CHUNK * j : CHUNK * (j + 1)] = g[4 * a : 4 * (a + 1)]
    spray(8, nd, d, dev_d, lambda q: h_send.at[q], h_recv)
    h_recv[d] = h_send[d]
    gb_recv[p] = gb_send[p]
    gather_wait(recv, 7, npa, gb_recv)
    hb_send[...] = jnp.sum(gb_recv[:, 0:2, :], axis=0)
    spray(9, nd, d, dev_d, lambda q: hb_send, hb_recv)
    hb_recv[d] = hb_send[...]

    gather_wait(recv, 5, npd, sv_recv)
    sw_recv[v] = jnp.sum(sv_recv[...], axis=0)
    spray(6, nv, v, dev_v, lambda q: sw_recv.at[v], sw_recv)

    gather_wait(recv, 8, nd, h_recv)
    dw = jnp.sum(h_recv[...], axis=0)
    for k in range(2):
        dw_ref[:, width * k : width * (k + 1)] = dw[2 * k : 2 * k + 2]
    gather_wait(recv, 9, nd, hb_recv)
    db = jnp.sum(hb_recv[...], axis=0)
    step = 128 // nd
    out = db[:, 0:step]
    for a in range(1, nd):
        out = jnp.where(
            jnp.full(out.shape, d, jnp.int32) == a, db[:, step * a : step * (a + 1)], out
        )
    db_ref[...] = out

    gather_wait(recv, 6, nv, sw_recv)
    du_ref[...] = sw_recv[...]

    gather_wait(send, 0, npd, wbuf)
    gather_wait(send, 1, nv, obuf)
    gather_wait(send, 2, nv, st_recv)
    gather_wait(send, 3, nv, res)
    gather_wait(send, 4, nv, su_recv)
    gather_wait(send, 5, npd, sv_recv)
    gather_wait(send, 6, nv, sw_recv)
    gather_wait(send, 7, npa, gb_recv)
    gather_wait(send, 8, nd, h_recv)
    gather_wait(send, 9, nd, hb_recv)
    for j in range(width // CHUNK):
        gather_wait(send, 10 + j, npa, g_recv.at[j])


def shards(
    sizes, pixels, emb_weight, chan_bias, score_vecs, value_weight, out_grad, slot_order
):
    nv, npa, nd = sizes
    npd = npa * nd
    samples, ch_dev, pix, patches = pixels.shape
    width, heads = score_vecs.shape
    channels = nv * ch_dev - nv // 4
    rows, cols = pix * ch_dev, samples * patches
    per = pix // npd
    pix_rows = pixels.transpose(2, 1, 3, 0).reshape(rows, cols)
    wblk = (
        emb_weight.reshape(ch_dev, per, 4, width // 4)
        .transpose(2, 1, 0, 3)
        .reshape(4 * per * ch_dev, width // 4)
    )
    og = out_grad.reshape(samples, width)
    vmem = pl.BlockSpec(memory_space=pltpu.VMEM)
    chunks = width // CHUNK
    tall = rows + 16
    dw, db, du = pl.pallas_call(
        functools.partial(kernel, (nv, npa, nd, channels)),
        out_shape=(
            jax.ShapeDtypeStruct((ch_dev, per * width), F32),
            jax.ShapeDtypeStruct((ch_dev, width // npd), F32),
            jax.ShapeDtypeStruct((heads, width // 128, 128), F32),
        ),
        in_specs=[pl.BlockSpec(memory_space=pltpu.SMEM)]
        + [vmem] * 5
        + [pl.BlockSpec(memory_space=pl.ANY)],
        out_specs=(vmem, vmem, vmem),
        scratch_shapes=[
            pltpu.VMEM((width, width), BF16),
            pltpu.VMEM((tall, 2 * cols), BF16),
            pltpu.VMEM((npd, 16, width // 4), BF16),
            pltpu.VMEM((tall, width), F32),
            pltpu.VMEM((nv, samples, width), BF16),
            pltpu.VMEM((2 * cols, width), BF16),
            pltpu.VMEM((width, 128), BF16),
            pltpu.VMEM((width, 128), BF16),
            pltpu.VMEM((128, width), BF16),
            pltpu.VMEM((128, width), BF16),
            pltpu.VMEM((2 * cols, 128), F32),
            pltpu.VMEM((2 * cols, width), BF16),
            pltpu.VMEM((nv, 8, 128), F32),
            pltpu.VMEM((nv, 8, 128), F32),
            pltpu.VMEM((nv, 8, 128), F32),
            pltpu.VMEM((3, heads, cols), F32),
            pltpu.VMEM((nv, 8, 128), F32),
            pltpu.VMEM((nv, 8, 128), F32),
            pltpu.VMEM((8, 128), F32),
            pltpu.VMEM((npd, 8, 128), F32),
            pltpu.VMEM((nv, 8, 128), F32),
            pltpu.VMEM((chunks, npa, 16, CHUNK), F32),
            pltpu.VMEM((chunks, npa, 16, CHUNK), F32),
            pltpu.VMEM((npa, 8, 128), F32),
            pltpu.VMEM((npa, 8, 128), F32),
            pltpu.VMEM((nd, 4, width), F32),
            pltpu.VMEM((nd, 4, width), F32),
            pltpu.VMEM((2, 128), F32),
            pltpu.VMEM((nd, 2, 128), F32),
            pltpu.SemaphoreType.DMA,
            pltpu.SemaphoreType.DMA((10 + chunks,)),
            pltpu.SemaphoreType.DMA((10 + chunks,)),
        ],
        compiler_params=pltpu.CompilerParams(
            collective_id=0, has_side_effects=True, vmem_limit_bytes=48 * 1024 * 1024
        ),
        name="backward",
    )(slot_order, pix_rows, wblk, chan_bias, score_vecs, og, value_weight)
    return dw, db, du.reshape(heads, width).T


def solution(mesh):
    sizes = (mesh.shape["var"], mesh.shape["patch"], mesh.shape["dp"])
    in_specs = (
        P("dp", "var", None, "patch"),
        P("var", ("patch", "dp")),
        P("var", None),
        P(),
        P(),
        P("dp", ("patch", "var"), None),
        P(),
    )
    out_specs = (P("var", ("patch", "dp")), P("var", ("patch", "dp")), P())
    return jax.shard_map(
        functools.partial(shards, sizes),
        mesh=mesh,
        in_specs=in_specs,
        out_specs=out_specs,
        check_vma=False,
    )
```

```python
import functools

import jax
import jax.numpy as jnp
from jax import lax
from jax.experimental import pallas as pl
from jax.experimental.pallas import tpu as pltpu
from jax.sharding import PartitionSpec as P

MESH = pl.DeviceIdType.MESH
F32 = jnp.float32
BF16 = jnp.bfloat16
CHUNK = 256
NEAR = (1, 7, 2, 6, 3, 5, 4)


def mm(a, b, ca=1, cb=0):
    return lax.dot_general(
        a, b, (((ca,), (cb,)), ((), ())), preferred_element_type=F32
    )


def iota(shape, dim):
    return lax.broadcasted_iota(jnp.int32, shape, dim)


def one_hot(cond):
    return jnp.where(cond, 1.0, 0.0).astype(BF16)


def kernel(
    sizes,
    slot_hbm,
    pix_hbm,
    emb_hbm,
    bias_hbm,
    vecs_hbm,
    og_hbm,
    value_hbm,
    dw_ref,
    db_ref,
    du_ref,
    slots,
    pix,
    emb,
    bias,
    vecs,
    wv,
    mts,
    mg,
    wtmp,
    wsend,
    wbuf,
    obuf,
    tok,
    spread,
    ut,
    zx,
    act,
    st_send,
    st_recv,
    res,
    stat,
    su_send,
    su_recv,
    sv_send,
    sv_recv,
    sw_recv,
    g_send,
    g_recv,
    gb_send,
    gb_recv,
    h_send,
    h_recv,
    hb_send,
    hb_recv,
    sem_in,
    sem_og,
    send,
    recv,
):
    nv, npa, nd, channels = sizes
    npd = npa * nd
    nchip = npd // 2
    heads = nv
    nz = len(NEAR) + 1
    v = lax.axis_index("var")
    p = lax.axis_index("patch")
    d = lax.axis_index("dp")
    pd = p * nd + d
    core = lax.rem(p, 2)
    chip = (p // 2) * nd + d
    y, z = v // nz, lax.rem(v, nz)
    width = wv.shape[0]
    hd = width // heads
    rows = mts.shape[1]
    cols = rows // 2
    chunks = width // CHUNK

    fetch = [
        pltpu.make_async_copy(src, dst, sem_in.at[i])
        for i, (src, dst) in enumerate(
            (
                (emb_hbm, emb),
                (og_hbm, obuf.at[v]),
                (pix_hbm, pix),
                (vecs_hbm, vecs),
                (bias_hbm, bias),
                (slot_hbm, slots),
                (value_hbm, wv),
            )
        )
    ]
    for copy in fetch:
        copy.start()

    def dev_v(q):
        return {"var": q}

    def dev_pd(q):
        return {"patch": q // nd, "dp": lax.rem(q, nd)}

    def dev_chip(q):
        return {"patch": (q // nd) * 2 + core, "dp": lax.rem(q, nd)}

    def dev_p(q):
        return {"patch": q}

    def dev_d(q):
        return {"dp": q}

    barrier = pltpu.get_barrier_semaphore()

    def greet(count, me, dev):
        def one(j, carry):
            pl.semaphore_signal(
                barrier,
                inc=1,
                device_id=dev(lax.rem(me + j, count)),
                device_id_type=MESH,
            )
            return carry

        lax.fori_loop(1, count, one, 0)

    greet(npd, pd, dev_pd)
    greet(nv, v, dev_v)

    def put(src, dst, send_sem, recv_sem, dev):
        pltpu.make_async_remote_copy(
            src_ref=src,
            dst_ref=dst,
            send_sem=send_sem,
            recv_sem=recv_sem,
            device_id=dev,
            device_id_type=MESH,
        ).start()

    def spray(k, count, me, dev, src, dst):
        def one(j, carry):
            q = lax.rem(me + j, count)
            put(src(q), dst.at[me], send.at[k], recv.at[k], dev(q))
            return carry

        lax.fori_loop(1, count, one, 0)

    def arrived(part, sem):
        pltpu.make_async_copy(part, part, sem).wait()

    def gather_wait(sems, k, count, dst):
        arrived(dst.at[pl.ds(0, count - 1)], sems.at[k])

    fetch[0].wait()
    block = emb[...].astype(F32)
    cw = wtmp.shape[1]
    for cc in range(4):
        for k in range(2):
            at = k * width + cc * cw
            wtmp[4 * cc + 2 * k : 4 * cc + 2 * k + 2, :] = block[:, at : at + cw]
    wsend[...] = wtmp[...].astype(BF16)
    fetch[1].wait()

    pl.semaphore_wait(barrier, nv - 1 + npd - 1)

    own = core * nchip + chip
    spray_slot = wbuf.at[own]

    def send_block(j, carry):
        q = lax.rem(chip + j, nchip)
        put(wsend, spray_slot, send.at[0], recv.at[0], dev_chip(q))
        return carry

    lax.fori_loop(1, nchip, send_block, 0)

    def pass_on(u):
        put(
            obuf.at[u],
            obuf.at[u],
            send.at[1],
            sem_og.at[u],
            dev_v(lax.rem(v + nz, nv)),
        )

    pass_on(v)
    for dz in reversed(NEAR):
        u = y * nz + lax.rem(z + dz, nz)
        put(obuf.at[v], obuf.at[v], send.at[1], sem_og.at[v], dev_v(u))
    wbuf[own] = wsend[...]

    def relay(dz):
        u = y * nz + lax.rem(z + dz, nz)
        arrived(obuf.at[u], sem_og.at[u])
        pass_on(u)

    fetch[2].wait()
    to = iota((rows, rows), 0)
    src = lax.rem(to, 16) * 32 + (to // cols) * 16 + lax.rem(to, cols) // 16
    pixp = mm(one_hot(iota((rows, rows), 1) == src), pix[...]).astype(BF16)
    npix = pixp.shape[1]
    col = iota((npix, rows), 1)
    slot = col // 16
    owner = (2 * (lax.rem(slot, nchip) // nd) + slot // nchip) * nd + lax.rem(slot, nd)
    of_pix = 2 * owner + lax.rem(col, 4) // 2 == iota((npix, rows), 0)
    same = lax.rem(iota((rows, rows), 1), 2) == to // cols
    relay(NEAR[0])
    relay(NEAR[1])
    for cc in range(4):
        pick = one_hot(of_pix & (lax.rem(col, 16) // 4 == cc))
        mts[cc] = jnp.where(same, mm(pixp, pick), 0.0).astype(BF16)
    relay(NEAR[2])
    relay(NEAR[3])
    nk = 2 * npix
    pick = one_hot(iota((nk, npix), 0) // 2 == iota((nk, npix), 1))
    mg[0:nk, :] = jnp.where(
        lax.rem(iota((nk, rows), 0), 2) == iota((nk, rows), 1) // cols,
        mm(pick, pixp, 1, 1),
        0.0,
    ).astype(BF16)
    tail = mg.shape[0] - nk
    mg[nk:, :] = one_hot(iota((tail, rows), 0) == iota((tail, rows), 1) // cols)
    fetch[3].wait()
    ut[...] = jnp.zeros(ut.shape, BF16)
    ut[heads : 2 * heads, :] = vecs[...]
    spread[...] = one_hot(iota((128, width), 1) // hd == iota((128, width), 0))
    relay(NEAR[4])
    relay(NEAR[5])
    fetch[4].wait()
    fetch[5].wait()

    gather_wait(recv, 0, nchip, wbuf)
    slab = wbuf.at[pl.ds(core * nchip, nchip)]
    put(slab, slab, send.at[2], recv.at[2], dev_p(p + 1 - 2 * core))
    relay(NEAR[6])
    arrived(slab, recv.at[2])

    blocks = wbuf[...].reshape(npd * 16, cw)
    for cc in range(4):
        sl = slice(cw * cc, cw * (cc + 1))
        t = mm(mts[cc], blocks)
        b = bias[:, sl].astype(F32)
        tok[0:cols, sl] = (t[0:cols] + b[0:1]).astype(BF16)
        tok[cols:, sl] = (t[cols:] + b[1:2]).astype(BF16)

    zx[...] = mm(tok[...], ut[...], 1, 1)
    fetch[6].wait()

    def other_row(j, carry):
        u = (1 - y) * nz + j
        arrived(obuf.at[u], sem_og.at[u])
        return carry

    lax.fori_loop(0, nz, other_row, 0)

    def products(j, carry):
        at = pl.multiple_of(j * CHUNK, CHUNK)
        vals = mm(tok[...], wv[:, pl.ds(at, CHUNK)])
        grad = obuf[:, :, pl.ds(at, CHUNK)].astype(F32).reshape(cols, CHUNK)
        prod = vals * jnp.concatenate([grad, grad], axis=0)
        hi = prod.astype(BF16)
        lo = (prod - hi.astype(F32)).astype(BF16)
        part = spread[:, pl.ds(at, CHUNK)]
        zx[...] += mm(hi, part, 1, 1) + mm(lo, part, 1, 1)
        return carry

    lax.fori_loop(0, chunks, products, 0)
    xt = jnp.transpose(zx[...])
    sc, dp = [], []
    for c in range(2):
        s = xt[heads : 2 * heads, cols * c : cols * (c + 1)]
        which = jnp.full(s.shape, slots[2 * v + c], jnp.int32)
        sc.append(jnp.where(which < channels, s, -1e30))
        dp.append(xt[0:heads, cols * c : cols * (c + 1)])

    top = jnp.maximum(sc[0], sc[1])
    e0, e1 = jnp.exp(sc[0] - top), jnp.exp(sc[1] - top)
    total = e0 + e1
    mean = (e0 * dp[0] + e1 * dp[1]) / total
    logsum = top + jnp.log(total)
    for h in range(heads):
        for k, x in enumerate((logsum, mean)):
            st_send[h, 2 * k : 2 * k + 1, :] = x[h : h + 1, 0:128]
            st_send[h, 2 * k + 1 : 2 * k + 2, :] = x[h : h + 1, 128:256]
    spray(3, nv, v, dev_v, lambda q: st_send.at[q], st_recv)
    st_recv[v] = st_send[v]
    gather_wait(recv, 3, nv, st_recv)
    got = st_recv[...]
    logs = got[:, 0:2, :]
    peak = jnp.max(logs, axis=0)
    scale = jnp.exp(logs - peak[None])
    total = jnp.sum(scale, axis=0)
    res[v, 0:2, :] = peak + jnp.log(total)
    res[v, 2:4, :] = jnp.sum(scale * got[:, 2:4, :], axis=0) / total
    spray(4, nv, v, dev_v, lambda q: res.at[v], res)
    gather_wait(recv, 4, nv, res)
    for h in range(heads):
        for k in range(2):
            stat[k, h : h + 1, 0:128] = res[h, 2 * k : 2 * k + 1, :]
            stat[k, h : h + 1, 128:256] = res[h, 2 * k + 1 : 2 * k + 2, :]
    logsum, mean = stat[0], stat[1]
    probs = [jnp.exp(s - logsum) for s in sc]
    dscore = jnp.concatenate([a * (b - mean) for a, b in zip(probs, dp)], axis=1)
    probs = jnp.concatenate(probs, axis=1)

    part = mm(dscore.astype(BF16), tok[...])
    for h in range(heads):
        for k in range(width // 128):
            su_send[h, k : k + 1, :] = part[h : h + 1, 128 * k : 128 * (k + 1)]
    spray(5, nv, v, dev_v, lambda q: su_send.at[q], su_recv)
    su_recv[v] = su_send[v]

    pad = jnp.zeros((128 - 2 * heads, rows), F32)
    q = jnp.transpose(jnp.concatenate([probs, dscore, pad], axis=0)).astype(BF16)
    grad = obuf[...].reshape(cols, width)
    for j in range(chunks):
        sl = slice(CHUNK * j, CHUNK * (j + 1))
        g = grad[:, sl].astype(F32)
        g = jnp.concatenate([g, g], axis=0)
        act[:, sl] = (mm(q, spread[:, sl]) * g).astype(BF16)
    for j in range(chunks):
        sl = slice(CHUNK * j, CHUNK * (j + 1))
        tg = (mm(act[...], wv[sl, :], 1, 1) + mm(q, ut[:, sl])).astype(BF16)
        g = mm(mg[...], tg)
        for a in range(npa):
            g_send[j, a] = g[16 * a : 16 * (a + 1)]
        for a in range(CHUNK // 128):
            gb_send[j * (CHUNK // 128) + a] = g[nk : nk + 2, 128 * a : 128 * (a + 1)]
        spray(11 + j, npa, p, dev_p, lambda q, j=j: g_send.at[j, q], g_recv.at[j])
    spray(8, npa, p, dev_p, lambda q: gb_send.at[q], gb_recv)

    gather_wait(recv, 5, nv, su_recv)
    su = jnp.sum(su_recv[...], axis=0)
    sv_send[...] = su
    spray(6, npd, pd, dev_pd, lambda q: sv_send, sv_recv)
    sv_recv[pd] = su

    for j in range(chunks):
        g_recv[j, p] = g_send[j, p]
        gather_wait(recv, 11 + j, npa, g_recv.at[j])
        g = jnp.sum(g_recv[j], axis=0)
        for a in range(nd):
            h_send[a, :, CHUNK * j : CHUNK * (j + 1)] = g[4 * a : 4 * (a + 1)]
    spray(9, nd, d, dev_d, lambda q: h_send.at[q], h_recv)
    h_recv[d] = h_send[d]
    gb_recv[p] = gb_send[p]
    gather_wait(recv, 8, npa, gb_recv)
    hb_send[...] = jnp.sum(gb_recv[...], axis=0)
    spray(10, nd, d, dev_d, lambda q: hb_send, hb_recv)
    hb_recv[d] = hb_send[...]

    gather_wait(recv, 6, npd, sv_recv)
    sw_recv[v] = jnp.sum(sv_recv[...], axis=0)
    spray(7, nv, v, dev_v, lambda q: sw_recv.at[v], sw_recv)

    gather_wait(recv, 9, nd, h_recv)
    dw = jnp.sum(h_recv[...], axis=0)
    for k in range(2):
        dw_ref[:, width * k : width * (k + 1)] = dw[2 * k : 2 * k + 2]
    gather_wait(recv, 10, nd, hb_recv)
    db = jnp.sum(hb_recv[...], axis=0)
    step = 128 // nd
    out = db[:, 0:step]
    for a in range(1, nd):
        mine = jnp.full(out.shape, d, jnp.int32) == a
        out = jnp.where(mine, db[:, step * a : step * (a + 1)], out)
    db_ref[...] = out

    gather_wait(send, 0, nchip, wbuf)
    gather_wait(send, 1, nv, obuf)
    arrived(slab, send.at[2])
    gather_wait(send, 3, nv, st_recv)
    gather_wait(send, 4, nv, res)
    gather_wait(send, 5, nv, su_recv)
    gather_wait(send, 6, npd, sv_recv)
    gather_wait(send, 8, npa, gb_recv)
    gather_wait(send, 9, nd, h_recv)
    gather_wait(send, 10, nd, hb_recv)
    for j in range(chunks):
        gather_wait(send, 11 + j, npa, g_recv.at[j])
    gather_wait(recv, 7, nv, sw_recv)
    du_ref[...] = sw_recv[...]
    gather_wait(send, 7, nv, sw_recv)


def shards(
    sizes, pixels, emb_weight, chan_bias, score_vecs, value_weight, out_grad, slot_order
):
    nv, npa, nd = sizes
    npd = npa * nd
    samples, ch_dev, npix, patches = pixels.shape
    width, heads = score_vecs.shape
    channels = nv * ch_dev - nv // 4
    rows = samples * patches * ch_dev
    per = npix // npd
    pix = pixels.transpose(0, 1, 3, 2).reshape(rows, npix)
    og = out_grad.reshape(samples, width)
    vmem = pl.BlockSpec(memory_space=pltpu.VMEM)
    chunks = width // CHUNK
    dw, db, du = pl.pallas_call(
        functools.partial(kernel, (nv, npa, nd, channels)),
        out_shape=(
            jax.ShapeDtypeStruct((ch_dev, per * width), F32),
            jax.ShapeDtypeStruct((ch_dev, width // npd), F32),
            jax.ShapeDtypeStruct((heads, width // 128, 128), F32),
        ),
        in_specs=[pl.BlockSpec(memory_space=pltpu.HBM)] * 7,
        out_specs=(vmem, vmem, vmem),
        scratch_shapes=[
            pltpu.SMEM(slot_order.shape, jnp.int32),
            pltpu.VMEM((rows, npix), BF16),
            pltpu.VMEM((ch_dev, per * width), BF16),
            pltpu.VMEM((ch_dev, width), BF16),
            pltpu.VMEM((heads, width), BF16),
            pltpu.VMEM((width, width), BF16),
            pltpu.VMEM((4, rows, npd * 16), BF16),
            pltpu.VMEM((npix * ch_dev + 16, rows), BF16),
            pltpu.VMEM((16, width // 4), F32),
            pltpu.VMEM((16, width // 4), BF16),
            pltpu.VMEM((npd, 16, width // 4), BF16),
            pltpu.VMEM((nv, samples, width), BF16),
            pltpu.VMEM((rows, width), BF16),
            pltpu.VMEM((128, width), BF16),
            pltpu.VMEM((128, width), BF16),
            pltpu.VMEM((rows, 128), F32),
            pltpu.VMEM((rows, width), BF16),
            pltpu.VMEM((nv, 4, 128), F32),
            pltpu.VMEM((nv, 4, 128), F32),
            pltpu.VMEM((nv, 4, 128), F32),
            pltpu.VMEM((2, heads, rows // 2), F32),
            pltpu.VMEM((nv, 8, 128), F32),
            pltpu.VMEM((nv, 8, 128), F32),
            pltpu.VMEM((8, 128), F32),
            pltpu.VMEM((npd, 8, 128), F32),
            pltpu.VMEM((nv, 8, 128), F32),
            pltpu.VMEM((chunks, npa, 16, CHUNK), F32),
            pltpu.VMEM((chunks, npa, 16, CHUNK), F32),
            pltpu.VMEM((npa, 2, 128), F32),
            pltpu.VMEM((npa, 2, 128), F32),
            pltpu.VMEM((nd, 4, width), F32),
            pltpu.VMEM((nd, 4, width), F32),
            pltpu.VMEM((2, 128), F32),
            pltpu.VMEM((nd, 2, 128), F32),
            pltpu.SemaphoreType.DMA((7,)),
            pltpu.SemaphoreType.DMA((nv,)),
            pltpu.SemaphoreType.DMA((11 + chunks,)),
            pltpu.SemaphoreType.DMA((11 + chunks,)),
        ],
        compiler_params=pltpu.CompilerParams(
            collective_id=0, has_side_effects=True, vmem_limit_bytes=60 * 1024 * 1024
        ),
        name="backward",
    )(slot_order, pix, emb_weight, chan_bias, score_vecs.T, og, value_weight)
    return dw, db, du.reshape(heads, width).T


def solution(mesh):
    sizes = (mesh.shape["var"], mesh.shape["patch"], mesh.shape["dp"])
    in_specs = (
        P("dp", "var", None, "patch"),
        P("var", ("patch", "dp")),
        P("var", None),
        P(),
        P(),
        P("dp", ("patch", "var"), None),
        P(),
    )
    out_specs = (P("var", ("patch", "dp")), P("var", ("patch", "dp")), P())
    return jax.shard_map(
        functools.partial(shards, sizes),
        mesh=mesh,
        in_specs=in_specs,
        out_specs=out_specs,
        check_vma=False,
    )
```

```python
import functools

import jax
import jax.numpy as jnp
from jax import lax
from jax.experimental import pallas as pl
from jax.experimental.pallas import tpu as pltpu
from jax.sharding import PartitionSpec as P

MESH = pl.DeviceIdType.MESH
F32 = jnp.float32
BF16 = jnp.bfloat16
CHUNK = 256
NEAR = (1, 7, 2, 6, 3, 5, 4)


def mm(a, b, ca=1, cb=0):
    return lax.dot_general(
        a, b, (((ca,), (cb,)), ((), ())), preferred_element_type=F32
    )


def iota(shape, dim):
    return lax.broadcasted_iota(jnp.int32, shape, dim)


def one_hot(cond):
    return jnp.where(cond, 1.0, 0.0).astype(BF16)


def kernel(
    sizes,
    slot_hbm,
    pix_hbm,
    emb_hbm,
    bias_hbm,
    vecs_hbm,
    og_hbm,
    value_hbm,
    dw_ref,
    db_ref,
    du_ref,
    slots,
    pix,
    emb,
    bias,
    vecs,
    wv,
    mts,
    mg,
    wtmp,
    wsend,
    wbuf,
    obuf,
    tok,
    spread,
    ut,
    vals,
    zx,
    act,
    st_send,
    st_recv,
    res,
    stat,
    sp_send,
    sp_recv,
    su_send,
    su_recv,
    sv_send,
    sv_recv,
    dub,
    g_send,
    g_recv,
    gb_send,
    gb_recv,
    h_send,
    h_recv,
    hb_send,
    hb_recv,
    sem_in,
    sem_og,
    send,
    recv,
):
    nv, npa, nd, channels = sizes
    npd = npa * nd
    nchip = npd // 2
    heads = nv
    nz = len(NEAR) + 1
    v = lax.axis_index("var")
    p = lax.axis_index("patch")
    d = lax.axis_index("dp")
    core = lax.rem(p, 2)
    chip = (p // 2) * nd + d
    y, z = v // nz, lax.rem(v, nz)
    width = wv.shape[0]
    hd = width // heads
    rows = mts.shape[1]
    cols = rows // 2
    chunks = width // CHUNK

    fetch = [
        pltpu.make_async_copy(src, dst, sem_in.at[i])
        for i, (src, dst) in enumerate(
            (
                (emb_hbm, emb),
                (og_hbm, obuf.at[v]),
                (pix_hbm, pix),
                (vecs_hbm, vecs),
                (bias_hbm, bias),
                (slot_hbm, slots),
                (value_hbm, wv),
            )
        )
    ]
    for copy in fetch:
        copy.start()

    def dev_v(q):
        return {"var": q}

    def dev_chip(q):
        return {"patch": (q // nd) * 2 + core, "dp": lax.rem(q, nd)}

    def dev_p(q):
        return {"patch": q}

    def dev_d(q):
        return {"dp": q}

    barrier = pltpu.get_barrier_semaphore()

    def greet(count, me, dev):
        def one(j, carry):
            pl.semaphore_signal(
                barrier,
                inc=1,
                device_id=dev(lax.rem(me + j, count)),
                device_id_type=MESH,
            )
            return carry

        lax.fori_loop(1, count, one, 0)

    greet(nchip, chip, dev_chip)
    greet(nv, v, dev_v)
    for x in range(npa // 2):
        pl.semaphore_signal(
            barrier,
            inc=1,
            device_id=dev_p(2 * x + 1 - core),
            device_id_type=MESH,
        )

    def put(src, dst, send_sem, recv_sem, dev):
        pltpu.make_async_remote_copy(
            src_ref=src,
            dst_ref=dst,
            send_sem=send_sem,
            recv_sem=recv_sem,
            device_id=dev,
            device_id_type=MESH,
        ).start()

    def spray(k, count, me, dev, src, dst):
        def one(j, carry):
            q = lax.rem(me + j, count)
            put(src(q), dst.at[me], send.at[k], recv.at[k], dev(q))
            return carry

        lax.fori_loop(1, count, one, 0)

    def arrived(part, sem):
        pltpu.make_async_copy(part, part, sem).wait()

    def gather_wait(sems, k, count, dst):
        arrived(dst.at[pl.ds(0, count - 1)], sems.at[k])

    fetch[0].wait()
    block = emb[...].astype(F32)
    cw = wtmp.shape[1]
    for cc in range(4):
        for k in range(2):
            at = k * width + cc * cw
            wtmp[4 * cc + 2 * k : 4 * cc + 2 * k + 2, :] = block[:, at : at + cw]
    wsend[...] = wtmp[...].astype(BF16)
    fetch[1].wait()

    pl.semaphore_wait(barrier, nv - 1 + nchip - 1 + npa // 2)

    own = core * nchip + chip
    spray_slot = wbuf.at[own]

    def send_block(j, carry):
        q = lax.rem(chip + j, nchip)
        put(wsend, spray_slot, send.at[0], recv.at[0], dev_chip(q))
        return carry

    lax.fori_loop(1, nchip, send_block, 0)

    def pass_on(u):
        put(
            obuf.at[u],
            obuf.at[u],
            send.at[1],
            sem_og.at[u],
            dev_v(lax.rem(v + nz, nv)),
        )

    pass_on(v)
    for dz in NEAR:
        u = y * nz + lax.rem(z + dz, nz)
        put(obuf.at[v], obuf.at[v], send.at[1], sem_og.at[v], dev_v(u))
    wbuf[own] = wsend[...]

    def relay(dz):
        u = y * nz + lax.rem(z + dz, nz)
        arrived(obuf.at[u], sem_og.at[u])
        pass_on(u)

    fetch[2].wait()
    to = iota((rows, rows), 0)
    src = lax.rem(to, 16) * 32 + (to // cols) * 16 + lax.rem(to, cols) // 16
    pixp = mm(one_hot(iota((rows, rows), 1) == src), pix[...]).astype(BF16)
    npix = pixp.shape[1]
    col = iota((npix, rows), 1)
    slot = col // 16
    owner = (2 * (lax.rem(slot, nchip) // nd) + slot // nchip) * nd + lax.rem(slot, nd)
    of_pix = 2 * owner + lax.rem(col, 4) // 2 == iota((npix, rows), 0)
    same = lax.rem(iota((rows, rows), 1), 2) == to // cols
    relay(NEAR[0])
    relay(NEAR[1])
    for cc in range(4):
        pick = one_hot(of_pix & (lax.rem(col, 16) // 4 == cc))
        mts[cc] = jnp.where(same, mm(pixp, pick), 0.0).astype(BF16)
    relay(NEAR[2])
    relay(NEAR[3])
    nk = 2 * npix
    pick = one_hot(iota((nk, npix), 0) // 2 == iota((nk, npix), 1))
    mg[0:nk, :] = jnp.where(
        lax.rem(iota((nk, rows), 0), 2) == iota((nk, rows), 1) // cols,
        mm(pick, pixp, 1, 1),
        0.0,
    ).astype(BF16)
    tail = mg.shape[0] - nk
    mg[nk:, :] = one_hot(iota((tail, rows), 0) == iota((tail, rows), 1) // cols)
    fetch[3].wait()
    ut[...] = jnp.zeros(ut.shape, BF16)
    ut[heads : 2 * heads, :] = vecs[...]
    spread[...] = one_hot(iota((128, width), 1) // hd == iota((128, width), 0))
    fetch[4].wait()
    fetch[5].wait()
    fetch[6].wait()

    gather_wait(recv, 0, nchip, wbuf)
    slab = wbuf.at[pl.ds(core * nchip, nchip)]
    sibling = dev_p(p + 1 - 2 * core)
    put(slab, slab, send.at[2], recv.at[2], sibling)
    relay(NEAR[4])
    relay(NEAR[5])
    relay(NEAR[6])
    arrived(slab, recv.at[2])

    blocks = wbuf[...].reshape(npd * 16, cw)
    for cc in range(4):
        sl = slice(cw * cc, cw * (cc + 1))
        t = mm(mts[cc], blocks)
        b = bias[:, sl].astype(F32)
        tok[0:cols, sl] = (t[0:cols] + b[0:1]).astype(BF16)
        tok[cols:, sl] = (t[cols:] + b[1:2]).astype(BF16)

    zx[...] = mm(tok[...], ut[...], 1, 1)
    for j in range(chunks):
        sl = slice(CHUNK * j, CHUNK * (j + 1))
        vals[:, sl] = mm(tok[...], wv[:, sl])

    def other_row(j, carry):
        u = (1 - y) * nz + j
        arrived(obuf.at[u], sem_og.at[u])
        return carry

    lax.fori_loop(0, nz, other_row, 0)

    def products(j, carry):
        at = pl.multiple_of(j * CHUNK, CHUNK)
        grad = obuf[:, :, pl.ds(at, CHUNK)].astype(F32).reshape(cols, CHUNK)
        prod = vals[:, pl.ds(at, CHUNK)] * jnp.concatenate([grad, grad], axis=0)
        hi = prod.astype(BF16)
        lo = (prod - hi.astype(F32)).astype(BF16)
        part = spread[:, pl.ds(at, CHUNK)]
        zx[...] += mm(hi, part, 1, 1) + mm(lo, part, 1, 1)
        return carry

    lax.fori_loop(0, chunks, products, 0)
    xt = jnp.transpose(zx[...])
    sc, dp = [], []
    for c in range(2):
        s = xt[heads : 2 * heads, cols * c : cols * (c + 1)]
        which = jnp.full(s.shape, slots[2 * v + c], jnp.int32)
        sc.append(jnp.where(which < channels, s, -1e30))
        dp.append(xt[0:heads, cols * c : cols * (c + 1)])

    top = jnp.maximum(sc[0], sc[1])
    e0, e1 = jnp.exp(sc[0] - top), jnp.exp(sc[1] - top)
    total = e0 + e1
    mean = (e0 * dp[0] + e1 * dp[1]) / total
    logsum = top + jnp.log(total)
    for h in range(heads):
        for k, x in enumerate((logsum, mean)):
            st_send[h, 2 * k : 2 * k + 1, :] = x[h : h + 1, 0:128]
            st_send[h, 2 * k + 1 : 2 * k + 2, :] = x[h : h + 1, 128:256]
    spray(3, nv, v, dev_v, lambda q: st_send.at[q], st_recv)
    st_recv[v] = st_send[v]
    gather_wait(recv, 3, nv, st_recv)
    got = st_recv[...]
    logs = got[:, 0:2, :]
    peak = jnp.max(logs, axis=0)
    scale = jnp.exp(logs - peak[None])
    total = jnp.sum(scale, axis=0)
    res[v, 0:2, :] = peak + jnp.log(total)
    res[v, 2:4, :] = jnp.sum(scale * got[:, 2:4, :], axis=0) / total
    spray(4, nv, v, dev_v, lambda q: res.at[v], res)
    gather_wait(recv, 4, nv, res)
    for h in range(heads):
        for k in range(2):
            stat[k, h : h + 1, 0:128] = res[h, 2 * k : 2 * k + 1, :]
            stat[k, h : h + 1, 128:256] = res[h, 2 * k + 1 : 2 * k + 2, :]
    logsum, mean = stat[0], stat[1]
    probs = [jnp.exp(s - logsum) for s in sc]
    dscore = jnp.concatenate([a * (b - mean) for a, b in zip(probs, dp)], axis=1)
    probs = jnp.concatenate(probs, axis=1)

    part = mm(dscore.astype(BF16), tok[...])
    nq = width // 256
    for h in range(heads):
        for k in range(2 * nq):
            sp_send[k // nq, h, k % nq : k % nq + 1, :] = part[
                h : h + 1, 128 * k : 128 * (k + 1)
            ]
    put(sp_send.at[1 - core], sp_recv, send.at[8], recv.at[8], sibling)

    pad = jnp.zeros((128 - 2 * heads, rows), F32)
    q = jnp.transpose(jnp.concatenate([probs, dscore, pad], axis=0)).astype(BF16)
    grad = obuf[...].reshape(cols, width)
    for j in range(chunks):
        sl = slice(CHUNK * j, CHUNK * (j + 1))
        g = grad[:, sl].astype(F32)
        g = jnp.concatenate([g, g], axis=0)
        act[:, sl] = (mm(q, spread[:, sl]) * g).astype(BF16)
    arrived(sp_recv, recv.at[8])
    su_send[...] = sp_send[core] + sp_recv[...]
    spray(5, nv, v, dev_v, lambda q: su_send.at[q], su_recv)
    su_recv[v] = su_send[v]
    for j in range(chunks):
        sl = slice(CHUNK * j, CHUNK * (j + 1))
        tg = (mm(act[...], wv[sl, :], 1, 1) + mm(q, ut[:, sl])).astype(BF16)
        g = mm(mg[...], tg)
        for a in range(npa):
            g_send[j, a] = g[16 * a : 16 * (a + 1)]
        for a in range(CHUNK // 128):
            gb_send[j * (CHUNK // 128) + a] = g[nk : nk + 2, 128 * a : 128 * (a + 1)]
        spray(13 + j, npa, p, dev_p, lambda q, j=j: g_send.at[j, q], g_recv.at[j])
    spray(11, npa, p, dev_p, lambda q: gb_send.at[q], gb_recv)

    gather_wait(recv, 5, nv, su_recv)
    su = jnp.sum(su_recv[...], axis=0)
    sv_send[...] = su
    spray(6, nchip, chip, dev_chip, lambda q: sv_send, sv_recv)
    sv_recv[chip] = su

    for j in range(chunks):
        g_recv[j, p] = g_send[j, p]
        gather_wait(recv, 13 + j, npa, g_recv.at[j])
        g = jnp.sum(g_recv[j], axis=0)
        for a in range(nd):
            h_send[a, :, CHUNK * j : CHUNK * (j + 1)] = g[4 * a : 4 * (a + 1)]
    spray(9, nd, d, dev_d, lambda q: h_send.at[q], h_recv)
    h_recv[d] = h_send[d]
    gb_recv[p] = gb_send[p]
    gather_wait(recv, 11, npa, gb_recv)
    hb_send[...] = jnp.sum(gb_recv[...], axis=0)
    spray(10, nd, d, dev_d, lambda q: hb_send, hb_recv)
    hb_recv[d] = hb_send[...]

    gather_wait(recv, 6, nchip, sv_recv)
    half = dub.at[core]
    half[v] = jnp.sum(sv_recv[...], axis=0)
    spray(7, nv, v, dev_v, lambda q: half.at[v], half)

    gather_wait(recv, 9, nd, h_recv)
    dw = jnp.sum(h_recv[...], axis=0)
    for k in range(2):
        dw_ref[:, width * k : width * (k + 1)] = dw[2 * k : 2 * k + 2]
    gather_wait(recv, 10, nd, hb_recv)
    db = jnp.sum(hb_recv[...], axis=0)
    step = 128 // nd
    out = db[:, 0:step]
    for a in range(1, nd):
        mine = jnp.full(out.shape, d, jnp.int32) == a
        out = jnp.where(mine, db[:, step * a : step * (a + 1)], out)
    db_ref[...] = out

    gather_wait(send, 0, nchip, wbuf)
    gather_wait(send, 1, nv, obuf)
    arrived(slab, send.at[2])
    gather_wait(send, 3, nv, st_recv)
    gather_wait(send, 4, nv, res)
    gather_wait(send, 5, nv, su_recv)
    gather_wait(send, 6, nchip, sv_recv)
    arrived(sp_recv, send.at[8])
    gather_wait(send, 11, npa, gb_recv)
    gather_wait(send, 9, nd, h_recv)
    gather_wait(send, 10, nd, hb_recv)
    for j in range(chunks):
        gather_wait(send, 13 + j, npa, g_recv.at[j])
    gather_wait(recv, 7, nv, half)
    put(half, half, send.at[12], recv.at[12], sibling)
    gather_wait(send, 7, nv, half)
    arrived(half, recv.at[12])
    for h in range(heads):
        for k in range(2 * nq):
            du_ref[h : h + 1, 128 * k : 128 * (k + 1)] = dub[
                k // nq, h, k % nq : k % nq + 1, :
            ]
    arrived(half, send.at[12])


def store(a_ref, b_ref, c_ref, a_out, b_out, c_out, sem):
    pairs = ((a_ref, a_out), (b_ref, b_out), (c_ref, c_out))
    copies = [
        pltpu.make_async_copy(src, dst, sem.at[i]) for i, (src, dst) in enumerate(pairs)
    ]
    for copy in copies:
        copy.start()
    for copy in copies:
        copy.wait()


def shards(
    sizes, pixels, emb_weight, chan_bias, score_vecs, value_weight, out_grad, slot_order
):
    nv, npa, nd = sizes
    npd = npa * nd
    samples, ch_dev, npix, patches = pixels.shape
    width, heads = score_vecs.shape
    channels = nv * ch_dev - nv // 4
    rows = samples * patches * ch_dev
    per = npix // npd
    pix = pixels.transpose(0, 1, 3, 2).reshape(rows, npix)
    og = out_grad.reshape(samples, width)
    vmem = pl.BlockSpec(memory_space=pltpu.VMEM)
    chunks = width // CHUNK
    dw, db, du = pl.pallas_call(
        functools.partial(kernel, (nv, npa, nd, channels)),
        out_shape=(
            jax.ShapeDtypeStruct((ch_dev, per * width), F32),
            jax.ShapeDtypeStruct((ch_dev, width // npd), F32),
            jax.ShapeDtypeStruct((heads, width), F32),
        ),
        in_specs=[pl.BlockSpec(memory_space=pltpu.HBM)] * 7,
        out_specs=(vmem, vmem, vmem),
        scratch_shapes=[
            pltpu.SMEM(slot_order.shape, jnp.int32),
            pltpu.VMEM((rows, npix), BF16),
            pltpu.VMEM((ch_dev, per * width), BF16),
            pltpu.VMEM((ch_dev, width), BF16),
            pltpu.VMEM((heads, width), BF16),
            pltpu.VMEM((width, width), BF16),
            pltpu.VMEM((4, rows, npd * 16), BF16),
            pltpu.VMEM((npix * ch_dev + 16, rows), BF16),
            pltpu.VMEM((16, width // 4), F32),
            pltpu.VMEM((16, width // 4), BF16),
            pltpu.VMEM((npd, 16, width // 4), BF16),
            pltpu.VMEM((nv, samples, width), BF16),
            pltpu.VMEM((rows, width), BF16),
            pltpu.VMEM((128, width), BF16),
            pltpu.VMEM((128, width), BF16),
            pltpu.VMEM((rows, width), F32),
            pltpu.VMEM((rows, 128), F32),
            pltpu.VMEM((rows, width), BF16),
            pltpu.VMEM((nv, 4, 128), F32),
            pltpu.VMEM((nv, 4, 128), F32),
            pltpu.VMEM((nv, 4, 128), F32),
            pltpu.VMEM((2, heads, rows // 2), F32),
            pltpu.VMEM((2, nv, width // 256, 128), F32),
            pltpu.VMEM((nv, width // 256, 128), F32),
            pltpu.VMEM((nv, width // 256, 128), F32),
            pltpu.VMEM((nv, width // 256, 128), F32),
            pltpu.VMEM((width // 256, 128), F32),
            pltpu.VMEM((npd // 2, width // 256, 128), F32),
            pltpu.VMEM((2, nv, width // 256, 128), F32),
            pltpu.VMEM((chunks, npa, 16, CHUNK), F32),
            pltpu.VMEM((chunks, npa, 16, CHUNK), F32),
            pltpu.VMEM((npa, 2, 128), F32),
            pltpu.VMEM((npa, 2, 128), F32),
            pltpu.VMEM((nd, 4, width), F32),
            pltpu.VMEM((nd, 4, width), F32),
            pltpu.VMEM((2, 128), F32),
            pltpu.VMEM((nd, 2, 128), F32),
            pltpu.SemaphoreType.DMA((7,)),
            pltpu.SemaphoreType.DMA((nv,)),
            pltpu.SemaphoreType.DMA((13 + chunks,)),
            pltpu.SemaphoreType.DMA((13 + chunks,)),
        ],
        compiler_params=pltpu.CompilerParams(
            collective_id=0, has_side_effects=True, vmem_limit_bytes=40 * 1024 * 1024
        ),
        name="backward",
    )(*(pltpu.with_memory_space_constraint(x, pltpu.HBM) for x in (slot_order, pix, emb_weight, chan_bias, score_vecs.T, og, value_weight)))
    parts = (dw, db, du)
    hbm = pl.BlockSpec(memory_space=pltpu.HBM)
    dw, db, du = pl.pallas_call(
        store,
        out_shape=tuple(jax.ShapeDtypeStruct(x.shape, F32) for x in parts),
        in_specs=[vmem] * 3,
        out_specs=(hbm,) * 3,
        scratch_shapes=[pltpu.SemaphoreType.DMA((3,))],
        name="store",
    )(*parts)
    return dw, db, du.T


def solution(mesh):
    sizes = (mesh.shape["var"], mesh.shape["patch"], mesh.shape["dp"])
    in_specs = (
        P("dp", "var", None, "patch"),
        P("var", ("patch", "dp")),
        P("var", None),
        P(),
        P(),
        P("dp", ("patch", "var"), None),
        P(),
    )
    out_specs = (P("var", ("patch", "dp")), P("var", ("patch", "dp")), P())
    return jax.shard_map(
        functools.partial(shards, sizes),
        mesh=mesh,
        in_specs=in_specs,
        out_specs=out_specs,
        check_vma=False,
    )
```

```python
import functools

import jax
import jax.numpy as jnp
from jax import lax
from jax.experimental import pallas as pl
from jax.experimental.pallas import tpu as pltpu
from jax.sharding import PartitionSpec as P

MESH = pl.DeviceIdType.MESH
F32 = jnp.float32
BF16 = jnp.bfloat16
CHUNK = 256
FAR = (4, 3, 5, 2, 6, 1, 7)
NEAR_V = ((1, 2), (1, 6), (0, 2), (0, 6), (1, 1), (1, 7), (0, 1), (0, 7), (1, 0))
NEAR_CHIP = tuple((x, d) for x in (2, 1, 3, 0) for d in (1, 3, 0) if (x, d) != (0, 0))
OWN = ((0, 2), (0, 6), (0, 1), (0, 7), (1, 0))
RELAYS = (
    (0, 6, 0, 2),
    (0, 2, 1, 6),
    (0, 6, 0, 1),
    (0, 2, 0, 7),
    (0, 6, 1, 1),
    (0, 2, 1, 7),
    (1, 0, 0, 1),
    (1, 0, 0, 7),
    (0, 2, 1, 0),
    (0, 6, 1, 0),
)


def mm(a, b, ca=1, cb=0):
    return lax.dot_general(
        a, b, (((ca,), (cb,)), ((), ())), preferred_element_type=F32
    )


def iota(shape, dim):
    return lax.broadcasted_iota(jnp.int32, shape, dim)


def one_hot(cond):
    return jnp.where(cond, 1.0, 0.0).astype(BF16)


def kernel(
    sizes,
    slot_hbm,
    pix_hbm,
    emb_hbm,
    bias_hbm,
    vecs_hbm,
    og_hbm,
    value_hbm,
    dw_ref,
    db_ref,
    du_ref,
    slots,
    pix,
    emb,
    bias,
    vecs,
    wv,
    mts,
    mg,
    wtmp,
    wsend,
    wbuf,
    obuf,
    tok,
    spread,
    ut,
    vals,
    zx,
    act,
    st_send,
    st_recv,
    res,
    stat,
    su_send,
    su_recv,
    sp_send,
    sp_recv,
    sv_send,
    sv_recv,
    dub,
    g_send,
    g_recv,
    gb_send,
    gb_recv,
    h_send,
    h_recv,
    hb_send,
    hb_recv,
    sem_in,
    sem_og,
    sem_w,
    sem_ws,
    send,
    recv,
):
    nv, npa, nd, channels = sizes
    npd = npa * nd
    nchip = npd // 2
    heads = nv
    nz = len(FAR) + 1
    v = lax.axis_index("var")
    p = lax.axis_index("patch")
    d = lax.axis_index("dp")
    core = lax.rem(p, 2)
    x = p // 2
    nx = npa // 2
    chip = d * nx + x
    y, z = v // nz, lax.rem(v, nz)
    width = wv.shape[0]
    hd = width // heads
    rows = mts.shape[1]
    cols = rows // 2
    chunks = width // CHUNK

    fetch = [
        pltpu.make_async_copy(src, dst, sem_in.at[i])
        for i, (src, dst) in enumerate(
            (
                (emb_hbm, emb),
                (og_hbm, obuf.at[v]),
                (pix_hbm, pix),
                (vecs_hbm, vecs),
                (bias_hbm, bias),
                (slot_hbm, slots),
                (value_hbm, wv),
            )
        )
    ]
    def at_v(a, b):
        return lax.rem(y + a, 2) * nz + lax.rem(z + b, nz)

    def at_chip(a, b):
        return {"patch": lax.rem(x + a, nx) * 2 + core, "dp": lax.rem(d + b, nd)}

    def dev_p(q):
        return {"patch": q}

    def dev_d(q):
        return {"dp": q}

    sibling = dev_p(p + 1 - 2 * core)

    barrier = pltpu.get_barrier_semaphore()
    friends = [{"var": at_v(a, b)} for a, b in NEAR_V]
    friends += [at_chip(a, b) for a, b in NEAR_CHIP] + [sibling]
    for dev in friends:
        pl.semaphore_signal(barrier, inc=1, device_id=dev, device_id_type=MESH)
    for copy in fetch:
        copy.start()

    def put(src, dst, send_sem, recv_sem, dev):
        pltpu.make_async_remote_copy(
            src_ref=src,
            dst_ref=dst,
            send_sem=send_sem,
            recv_sem=recv_sem,
            device_id=dev,
            device_id_type=MESH,
        ).start()

    def spray(k, count, me, dev, src, dst):
        def one(j, carry):
            q = lax.rem(me + j, count)
            put(src(q), dst.at[me], send.at[k], recv.at[k], dev(q))
            return carry

        lax.fori_loop(1, count, one, 0)

    def spray_v(k, src, dst):
        for a, b in [(a, b) for b in FAR for a in (1, 0)] + [(1, 0)]:
            q = at_v(a, b)
            put(src(q), dst.at[v], send.at[k], recv.at[k], {"var": q})

    def spray_chip(k, src, dst):
        def one(j, carry):
            q = lax.rem(chip + j, nchip)
            to = {"patch": lax.rem(q, nx) * 2 + core, "dp": q // nx}
            put(src, dst.at[chip], send.at[k], recv.at[k], to)
            return carry

        lax.fori_loop(1, nchip, one, 0)

    def arrived(part, sem):
        pltpu.make_async_copy(part, part, sem).wait()

    def gather_wait(sems, k, count, dst):
        arrived(dst.at[pl.ds(0, count - 1)], sems.at[k])

    fetch[0].wait()
    block = emb[...].astype(F32)
    cw = wtmp.shape[1]
    for cc in range(4):
        for k in range(2):
            at = k * width + cc * cw
            wtmp[4 * cc + 2 * k : 4 * cc + 2 * k + 2, :] = block[:, at : at + cw]
    wsend[...] = wtmp[...].astype(BF16)
    fetch[1].wait()

    pl.semaphore_wait(barrier, len(friends))

    own = core * nchip + chip
    mine = obuf.at[v]
    for a, b in OWN:
        put(mine, mine, send.at[1], sem_og.at[v], {"var": at_v(a, b)})
    for a, b in NEAR_CHIP:
        put(wsend, wbuf.at[own], send.at[0], sem_w.at[d], at_chip(a, b))
    wbuf[own] = wsend[...]

    waited = set()

    def take(a, b):
        u = at_v(a, b)
        if (a, b) not in waited:
            waited.add((a, b))
            arrived(obuf.at[u], sem_og.at[u])
        return u

    def relay(oa, ob, a, b):
        u = take(oa, ob)
        put(obuf.at[u], obuf.at[u], send.at[1], sem_og.at[u], {"var": at_v(a, b)})

    def column(c, b):
        return wbuf.at[pl.ds(c * nchip + lax.rem(d + b, nd) * nx, nx)]

    def to_sibling(b):
        part = column(core, b)
        put(part, part, send.at[2], sem_ws.at[b], sibling)

    def take_column(b):
        part = column(core, b)
        arrived(part if b else part.at[pl.ds(0, nx - 1)], sem_w.at[lax.rem(d + b, nd)])
        to_sibling(b)

    fetch[2].wait()
    to = iota((rows, rows), 0)
    src = lax.rem(to, 16) * 32 + (to // cols) * 16 + lax.rem(to, cols) // 16
    pixp = mm(one_hot(iota((rows, rows), 1) == src), pix[...]).astype(BF16)
    npix = pixp.shape[1]
    col = iota((npix, rows), 1)
    slot = col // 16
    owner = 2 * lax.rem(slot, nx) + slot // nchip
    owner = owner * nd + lax.rem(slot, nchip) // nx
    of_pix = 2 * owner + lax.rem(col, 4) // 2 == iota((npix, rows), 0)
    same = lax.rem(iota((rows, rows), 1), 2) == to // cols
    for cc in range(2):
        pick = one_hot(of_pix & (lax.rem(col, 16) // 4 == cc))
        mts[cc] = jnp.where(same, mm(pixp, pick), 0.0).astype(BF16)
    for path in RELAYS[:6]:
        relay(*path)
    for cc in range(2, 4):
        pick = one_hot(of_pix & (lax.rem(col, 16) // 4 == cc))
        mts[cc] = jnp.where(same, mm(pixp, pick), 0.0).astype(BF16)
    take_column(1)
    part = column(core, 1)
    put(part, part, send.at[3], sem_w.at[lax.rem(d + 1, nd)], at_chip(0, nd - 1))
    for path in RELAYS[6:]:
        relay(*path)
    take_column(nd - 1)
    take_column(0)
    nk = 2 * npix
    pick = one_hot(iota((nk, npix), 0) // 2 == iota((nk, npix), 1))
    mg[0:nk, :] = jnp.where(
        lax.rem(iota((nk, rows), 0), 2) == iota((nk, rows), 1) // cols,
        mm(pick, pixp, 1, 1),
        0.0,
    ).astype(BF16)
    tail = mg.shape[0] - nk
    mg[nk:, :] = one_hot(iota((tail, rows), 0) == iota((tail, rows), 1) // cols)
    fetch[3].wait()
    ut[...] = jnp.zeros(ut.shape, BF16)
    ut[heads : 2 * heads, :] = vecs[...]
    spread[...] = one_hot(iota((128, width), 1) // hd == iota((128, width), 0))
    fetch[4].wait()
    fetch[5].wait()
    fetch[6].wait()

    take_column(2)
    for b in range(nd):
        arrived(column(1 - core, b), sem_ws.at[b])

    blocks = wbuf[...].reshape(npd * 16, cw)
    for cc in range(4):
        sl = slice(cw * cc, cw * (cc + 1))
        t = mm(mts[cc], blocks)
        b = bias[:, sl].astype(F32)
        tok[0:cols, sl] = (t[0:cols] + b[0:1]).astype(BF16)
        tok[cols:, sl] = (t[cols:] + b[1:2]).astype(BF16)

    zx[...] = mm(tok[...], ut[...], 1, 1)
    for j in range(chunks):
        sl = slice(CHUNK * j, CHUNK * (j + 1))
        vals[:, sl] = mm(tok[...], wv[:, sl])

    for a in range(2):
        for b in range(nz):
            if (a, b) != (0, 0):
                take(a, b)

    def products(j, carry):
        at = pl.multiple_of(j * CHUNK, CHUNK)
        grad = obuf[:, :, pl.ds(at, CHUNK)].astype(F32).reshape(cols, CHUNK)
        prod = vals[:, pl.ds(at, CHUNK)] * jnp.concatenate([grad, grad], axis=0)
        hi = prod.astype(BF16)
        lo = (prod - hi.astype(F32)).astype(BF16)
        part = spread[:, pl.ds(at, CHUNK)]
        zx[...] += mm(hi, part, 1, 1) + mm(lo, part, 1, 1)
        return carry

    lax.fori_loop(0, chunks, products, 0)
    xt = jnp.transpose(zx[...])
    sc, dp = [], []
    for c in range(2):
        s = xt[heads : 2 * heads, cols * c : cols * (c + 1)]
        which = jnp.full(s.shape, slots[2 * v + c], jnp.int32)
        sc.append(jnp.where(which < channels, s, -1e30))
        dp.append(xt[0:heads, cols * c : cols * (c + 1)])

    top = jnp.maximum(sc[0], sc[1])
    e0, e1 = jnp.exp(sc[0] - top), jnp.exp(sc[1] - top)
    total = e0 + e1
    mean = (e0 * dp[0] + e1 * dp[1]) / total
    logsum = top + jnp.log(total)
    for h in range(heads):
        for k, x in enumerate((logsum, mean)):
            st_send[h, 2 * k : 2 * k + 1, :] = x[h : h + 1, 0:128]
            st_send[h, 2 * k + 1 : 2 * k + 2, :] = x[h : h + 1, 128:256]
    spray_v(4, lambda q: st_send.at[q], st_recv)
    st_recv[v] = st_send[v]
    gather_wait(recv, 4, nv, st_recv)
    got = st_recv[...]
    logs = got[:, 0:2, :]
    peak = jnp.max(logs, axis=0)
    scale = jnp.exp(logs - peak[None])
    total = jnp.sum(scale, axis=0)
    res[v, 0:2, :] = peak + jnp.log(total)
    res[v, 2:4, :] = jnp.sum(scale * got[:, 2:4, :], axis=0) / total
    spray_v(5, lambda q: res.at[v], res)
    gather_wait(recv, 5, nv, res)
    for h in range(heads):
        for k in range(2):
            stat[k, h : h + 1, 0:128] = res[h, 2 * k : 2 * k + 1, :]
            stat[k, h : h + 1, 128:256] = res[h, 2 * k + 1 : 2 * k + 2, :]
    logsum, mean = stat[0], stat[1]
    probs = [jnp.exp(s - logsum) for s in sc]
    dscore = jnp.concatenate([a * (b - mean) for a, b in zip(probs, dp)], axis=1)
    probs = jnp.concatenate(probs, axis=1)

    part = mm(dscore.astype(BF16), tok[...])
    nl = width // 128
    for h in range(heads):
        for k in range(nl):
            su_send[h, k : k + 1, :] = part[h : h + 1, 128 * k : 128 * (k + 1)]
    spray_v(6, lambda q: su_send.at[q], su_recv)
    su_recv[v] = su_send[v]

    pad = jnp.zeros((128 - 2 * heads, rows), F32)
    q = jnp.transpose(jnp.concatenate([probs, dscore, pad], axis=0)).astype(BF16)
    grad = obuf[...].reshape(cols, width)
    for j in range(chunks):
        sl = slice(CHUNK * j, CHUNK * (j + 1))
        g = grad[:, sl].astype(F32)
        g = jnp.concatenate([g, g], axis=0)
        act[:, sl] = (mm(q, spread[:, sl]) * g).astype(BF16)
    for j in range(chunks):
        sl = slice(CHUNK * j, CHUNK * (j + 1))
        tg = (mm(act[...], wv[sl, :], 1, 1) + mm(q, ut[:, sl])).astype(BF16)
        g = mm(mg[...], tg)
        for a in range(npa):
            g_send[j, a] = g[16 * a : 16 * (a + 1)]
        for a in range(CHUNK // 128):
            gb_send[j * (CHUNK // 128) + a] = g[nk : nk + 2, 128 * a : 128 * (a + 1)]
        spray(13 + j, npa, p, dev_p, lambda q, j=j: g_send.at[j, q], g_recv.at[j])
    spray(10, npa, p, dev_p, lambda q: gb_send.at[q], gb_recv)

    gather_wait(recv, 6, nv, su_recv)
    su = jnp.sum(su_recv[...], axis=0)
    sp_send[...] = su
    put(sp_send, sp_recv, send.at[7], recv.at[7], sibling)
    arrived(sp_recv, recv.at[7])
    sv_send[...] = su + sp_recv[...]
    spray_chip(8, sv_send, sv_recv)
    sv_recv[chip] = sv_send[...]

    for j in range(chunks):
        g_recv[j, p] = g_send[j, p]
        gather_wait(recv, 13 + j, npa, g_recv.at[j])
        g = jnp.sum(g_recv[j], axis=0)
        for a in range(nd):
            h_send[a, :, CHUNK * j : CHUNK * (j + 1)] = g[4 * a : 4 * (a + 1)]
    spray(11, nd, d, dev_d, lambda q: h_send.at[q], h_recv)
    h_recv[d] = h_send[d]
    gb_recv[p] = gb_send[p]
    gather_wait(recv, 10, npa, gb_recv)
    hb_send[...] = jnp.sum(gb_recv[...], axis=0)
    spray(12, nd, d, dev_d, lambda q: hb_send, hb_recv)
    hb_recv[d] = hb_send[...]

    gather_wait(recv, 8, nchip, sv_recv)
    dub[v] = jnp.sum(sv_recv[...], axis=0)
    spray_v(9, lambda q: dub.at[v], dub)

    gather_wait(recv, 11, nd, h_recv)
    dw = jnp.sum(h_recv[...], axis=0)
    for k in range(2):
        dw_ref[:, width * k : width * (k + 1)] = dw[2 * k : 2 * k + 2]
    gather_wait(recv, 12, nd, hb_recv)
    db = jnp.sum(hb_recv[...], axis=0)
    step = 128 // nd
    out = db[:, 0:step]
    for a in range(1, nd):
        mine = jnp.full(out.shape, d, jnp.int32) == a
        out = jnp.where(mine, db[:, step * a : step * (a + 1)], out)
    db_ref[...] = out

    arrived(wbuf.at[pl.ds(0, len(NEAR_CHIP))], send.at[0])
    gather_wait(send, 1, nv, obuf)
    arrived(wbuf.at[pl.ds(0, nchip)], send.at[2])
    arrived(wbuf.at[pl.ds(0, nx)], send.at[3])
    gather_wait(send, 4, nv, st_recv)
    gather_wait(send, 5, nv, res)
    gather_wait(send, 6, nv, su_recv)
    arrived(sp_recv, send.at[7])
    gather_wait(send, 8, nchip, sv_recv)
    gather_wait(send, 10, npa, gb_recv)
    gather_wait(send, 11, nd, h_recv)
    gather_wait(send, 12, nd, hb_recv)
    for j in range(chunks):
        gather_wait(send, 13 + j, npa, g_recv.at[j])
    gather_wait(recv, 9, nv, dub)
    for h in range(heads):
        for k in range(nl):
            du_ref[h : h + 1, 128 * k : 128 * (k + 1)] = dub[h, k : k + 1, :]
    gather_wait(send, 9, nv, dub)


def store(a_ref, b_ref, c_ref, a_out, b_out, c_out, sem):
    pairs = ((a_ref, a_out), (b_ref, b_out), (c_ref, c_out))
    copies = [
        pltpu.make_async_copy(src, dst, sem.at[i]) for i, (src, dst) in enumerate(pairs)
    ]
    for copy in copies:
        copy.start()
    for copy in copies:
        copy.wait()


def shards(
    sizes, pixels, emb_weight, chan_bias, score_vecs, value_weight, out_grad, slot_order
):
    nv, npa, nd = sizes
    npd = npa * nd
    samples, ch_dev, npix, patches = pixels.shape
    width, heads = score_vecs.shape
    channels = nv * ch_dev - nv // 4
    rows = samples * patches * ch_dev
    per = npix // npd
    pix = pixels.transpose(0, 1, 3, 2).reshape(rows, npix)
    og = out_grad.reshape(samples, width)
    vmem = pl.BlockSpec(memory_space=pltpu.VMEM)
    chunks = width // CHUNK
    dw, db, du = pl.pallas_call(
        functools.partial(kernel, (nv, npa, nd, channels)),
        out_shape=(
            jax.ShapeDtypeStruct((ch_dev, per * width), F32),
            jax.ShapeDtypeStruct((ch_dev, width // npd), F32),
            jax.ShapeDtypeStruct((heads, width), F32),
        ),
        in_specs=[pl.BlockSpec(memory_space=pltpu.HBM)] * 7,
        out_specs=(vmem, vmem, vmem),
        scratch_shapes=[
            pltpu.SMEM(slot_order.shape, jnp.int32),
            pltpu.VMEM((rows, npix), BF16),
            pltpu.VMEM((ch_dev, per * width), BF16),
            pltpu.VMEM((ch_dev, width), BF16),
            pltpu.VMEM((heads, width), BF16),
            pltpu.VMEM((width, width), BF16),
            pltpu.VMEM((4, rows, npd * 16), BF16),
            pltpu.VMEM((npix * ch_dev + 16, rows), BF16),
            pltpu.VMEM((16, width // 4), F32),
            pltpu.VMEM((16, width // 4), BF16),
            pltpu.VMEM((npd, 16, width // 4), BF16),
            pltpu.VMEM((nv, samples, width), BF16),
            pltpu.VMEM((rows, width), BF16),
            pltpu.VMEM((128, width), BF16),
            pltpu.VMEM((128, width), BF16),
            pltpu.VMEM((rows, width), F32),
            pltpu.VMEM((rows, 128), F32),
            pltpu.VMEM((rows, width), BF16),
            pltpu.VMEM((nv, 4, 128), F32),
            pltpu.VMEM((nv, 4, 128), F32),
            pltpu.VMEM((nv, 4, 128), F32),
            pltpu.VMEM((2, heads, rows // 2), F32),
            pltpu.VMEM((nv, width // 128, 128), F32),
            pltpu.VMEM((nv, width // 128, 128), F32),
            pltpu.VMEM((width // 128, 128), F32),
            pltpu.VMEM((width // 128, 128), F32),
            pltpu.VMEM((width // 128, 128), F32),
            pltpu.VMEM((npd // 2, width // 128, 128), F32),
            pltpu.VMEM((nv, width // 128, 128), F32),
            pltpu.VMEM((chunks, npa, 16, CHUNK), F32),
            pltpu.VMEM((chunks, npa, 16, CHUNK), F32),
            pltpu.VMEM((npa, 2, 128), F32),
            pltpu.VMEM((npa, 2, 128), F32),
            pltpu.VMEM((nd, 4, width), F32),
            pltpu.VMEM((nd, 4, width), F32),
            pltpu.VMEM((2, 128), F32),
            pltpu.VMEM((nd, 2, 128), F32),
            pltpu.SemaphoreType.DMA((7,)),
            pltpu.SemaphoreType.DMA((nv,)),
            pltpu.SemaphoreType.DMA((nd,)),
            pltpu.SemaphoreType.DMA((nd,)),
            pltpu.SemaphoreType.DMA((13 + chunks,)),
            pltpu.SemaphoreType.DMA((13 + chunks,)),
        ],
        compiler_params=pltpu.CompilerParams(
            collective_id=0, has_side_effects=True, vmem_limit_bytes=40 * 1024 * 1024
        ),
        name="backward",
    )(*(pltpu.with_memory_space_constraint(x, pltpu.HBM) for x in (slot_order, pix, emb_weight, chan_bias, score_vecs.T, og, value_weight)))
    parts = (dw, db, du)
    hbm = pl.BlockSpec(memory_space=pltpu.HBM)
    dw, db, du = pl.pallas_call(
        store,
        out_shape=tuple(jax.ShapeDtypeStruct(x.shape, F32) for x in parts),
        in_specs=[vmem] * 3,
        out_specs=(hbm,) * 3,
        scratch_shapes=[pltpu.SemaphoreType.DMA((3,))],
        compiler_params=pltpu.CompilerParams(vmem_limit_bytes=4 * 1024 * 1024),
        name="store",
    )(*parts)
    return dw, db, du.T


def solution(mesh):
    sizes = (mesh.shape["var"], mesh.shape["patch"], mesh.shape["dp"])
    in_specs = (
        P("dp", "var", None, "patch"),
        P("var", ("patch", "dp")),
        P("var", None),
        P(),
        P(),
        P("dp", ("patch", "var"), None),
        P(),
    )
    out_specs = (P("var", ("patch", "dp")), P("var", ("patch", "dp")), P())
    return jax.shard_map(
        functools.partial(shards, sizes),
        mesh=mesh,
        in_specs=in_specs,
        out_specs=out_specs,
        check_vma=False,
    )
```

```python
import functools

import jax
import jax.numpy as jnp
from jax import lax
from jax.experimental import pallas as pl
from jax.experimental.pallas import tpu as pltpu
from jax.sharding import PartitionSpec as P

MESH = pl.DeviceIdType.MESH
F32 = jnp.float32
BF16 = jnp.bfloat16
CHUNK = 256
FAR = (4, 3, 5, 2, 6, 1, 7)
NEAR_V = ((1, 2), (1, 6), (0, 2), (0, 6), (1, 1), (1, 7), (0, 1), (0, 7), (1, 0))
NEAR_CHIP = tuple((x, d) for x in (2, 1, 3, 0) for d in (1, 3, 0) if (x, d) != (0, 0))
PLACE = {0: 0, 1: 1, 3: 2, 2: 3}
OWN = ((0, 2), (0, 6), (0, 1), (0, 7), (1, 0))
RELAYS = (
    (0, 6, 0, 2),
    (0, 2, 1, 6),
    (0, 6, 0, 1),
    (0, 2, 0, 7),
    (0, 6, 1, 1),
    (0, 2, 1, 7),
    (1, 0, 0, 1),
    (1, 0, 0, 7),
    (0, 2, 1, 0),
    (0, 6, 1, 0),
)


def mm(a, b, ca=1, cb=0):
    return lax.dot_general(
        a, b, (((ca,), (cb,)), ((), ())), preferred_element_type=F32
    )


def iota(shape, dim):
    return lax.broadcasted_iota(jnp.int32, shape, dim)


def one_hot(cond):
    return jnp.where(cond, 1.0, 0.0).astype(BF16)


def kernel(
    sizes,
    slot_hbm,
    pix_hbm,
    emb_hbm,
    bias_hbm,
    vecs_hbm,
    og_hbm,
    value_hbm,
    dw_ref,
    db_ref,
    du_ref,
    slots,
    pix,
    emb,
    bias,
    vecs,
    wv,
    mts,
    mg,
    wtmp,
    wsend,
    wbuf,
    obuf,
    tok,
    spread,
    ut,
    vals,
    zx,
    act,
    st_send,
    st_recv,
    res,
    stat,
    su_send,
    su_recv,
    sp_send,
    sp_recv,
    sv_send,
    sv_recv,
    dub,
    g_send,
    g_recv,
    gb_send,
    gb_recv,
    h_send,
    h_recv,
    hb_send,
    hb_recv,
    sem_in,
    sem_og,
    sem_w,
    sem_ws,
    send,
    recv,
):
    nv, npa, nd, channels = sizes
    npd = npa * nd
    nchip = npd // 2
    heads = nv
    nz = len(FAR) + 1
    v = lax.axis_index("var")
    p = lax.axis_index("patch")
    d = lax.axis_index("dp")
    core = lax.rem(p, 2)
    x = p // 2
    nx = npa // 2
    chip = d * nx + x
    y, z = v // nz, lax.rem(v, nz)
    width = wv.shape[0]
    hd = width // heads
    rows = mts.shape[1]
    cols = rows // 2
    chunks = width // CHUNK

    fetch = [
        pltpu.make_async_copy(src, dst, sem_in.at[i])
        for i, (src, dst) in enumerate(
            (
                (emb_hbm, emb),
                (og_hbm, obuf.at[v]),
                (pix_hbm, pix),
                (vecs_hbm, vecs),
                (bias_hbm, bias),
                (slot_hbm, slots),
                (value_hbm, wv),
            )
        )
    ]
    def at_v(a, b):
        return lax.rem(y + a, 2) * nz + lax.rem(z + b, nz)

    def at_chip(a, b):
        return {"patch": lax.rem(x + a, nx) * 2 + core, "dp": lax.rem(d + b, nd)}

    def dev_p(q):
        return {"patch": q}

    def dev_d(q):
        return {"dp": q}

    sibling = dev_p(p + 1 - 2 * core)

    barrier = pltpu.get_barrier_semaphore()
    friends = [at_chip(a, b) for a, b in NEAR_CHIP]
    friends += [{"var": at_v(a, b)} for a, b in NEAR_V] + [sibling]
    for dev in friends:
        pl.semaphore_signal(barrier, inc=1, device_id=dev, device_id_type=MESH)
    for copy in fetch:
        copy.start()

    def put(src, dst, send_sem, recv_sem, dev):
        pltpu.make_async_remote_copy(
            src_ref=src,
            dst_ref=dst,
            send_sem=send_sem,
            recv_sem=recv_sem,
            device_id=dev,
            device_id_type=MESH,
        ).start()

    def spray(k, count, me, dev, src, dst):
        def one(j, carry):
            q = lax.rem(me + j, count)
            put(src(q), dst.at[me], send.at[k], recv.at[k], dev(q))
            return carry

        lax.fori_loop(1, count, one, 0)

    def spray_v(k, src, dst):
        for a, b in [(a, b) for b in FAR for a in (1, 0)] + [(1, 0)]:
            q = at_v(a, b)
            put(src(q), dst.at[v], send.at[k], recv.at[k], {"var": q})

    def spray_chip(k, src, dst):
        def one(j, carry):
            q = lax.rem(chip + j, nchip)
            to = {"patch": lax.rem(q, nx) * 2 + core, "dp": q // nx}
            put(src, dst.at[chip], send.at[k], recv.at[k], to)
            return carry

        lax.fori_loop(1, nchip, one, 0)

    def arrived(part, sem):
        pltpu.make_async_copy(part, part, sem).wait()

    def gather_wait(sems, k, count, dst):
        arrived(dst.at[pl.ds(0, count - 1)], sems.at[k])

    fetch[0].wait()
    block = emb[...].astype(F32)
    cw = wtmp.shape[1]
    for cc in range(4):
        for k in range(2):
            at = k * width + cc * cw
            wtmp[4 * cc + 2 * k : 4 * cc + 2 * k + 2, :] = block[:, at : at + cw]
    wsend[...] = wtmp[...].astype(BF16)

    pl.semaphore_wait(barrier, len(friends))

    mine = obuf.at[v]
    for a, b in NEAR_CHIP:
        slot = PLACE[-b % nd] * 2 * nx + core * nx + x
        put(wsend, wbuf.at[slot], send.at[0], sem_w.at[-b % nd], at_chip(a, b))
    fetch[1].wait()
    for a, b in OWN:
        put(mine, mine, send.at[1], sem_og.at[v], {"var": at_v(a, b)})
    wbuf[core * nx + x] = wsend[...]

    waited = set()

    def take(a, b):
        u = at_v(a, b)
        if (a, b) not in waited:
            waited.add((a, b))
            arrived(obuf.at[u], sem_og.at[u])
        return u

    def relay(oa, ob, a, b):
        u = take(oa, ob)
        put(obuf.at[u], obuf.at[u], send.at[1], sem_og.at[u], {"var": at_v(a, b)})

    def column(c, b):
        return wbuf.at[pl.ds((PLACE[b] * 2 + c) * nx, nx)]

    def to_sibling(b):
        part = column(core, b)
        put(part, part, send.at[2], sem_ws.at[b], sibling)

    def take_column(b):
        part = column(core, b)
        arrived(part if b else part.at[pl.ds(0, nx - 1)], sem_w.at[b])
        to_sibling(b)

    fetch[2].wait()
    to = iota((rows, rows), 0)
    src = lax.rem(to, 16) * 32 + (to // cols) * 16 + lax.rem(to, cols) // 16
    pixp = mm(one_hot(iota((rows, rows), 1) == src), pix[...]).astype(BF16)
    npix = pixp.shape[1]
    col = iota((npix, rows), 1)
    slot = col // 16
    place = slot // (2 * nx)
    offset = jnp.where(place == 2, 3, jnp.where(place == 3, 2, place))
    owner = 2 * lax.rem(slot, nx) + lax.rem(slot, 2 * nx) // nx
    owner = owner * nd + lax.rem(d + offset, nd)
    of_pix = 2 * owner + lax.rem(col, 4) // 2 == iota((npix, rows), 0)
    same = lax.rem(iota((rows, rows), 1), 2) == to // cols
    for cc in range(4):
        pick = one_hot(of_pix & (lax.rem(col, 16) // 4 == cc))
        mts[cc] = jnp.where(same, mm(pixp, pick), 0.0).astype(BF16)
    take_column(1)
    put(column(core, 1), column(core, 2), send.at[3], sem_w.at[2], at_chip(0, nd - 1))
    for path in RELAYS[:6]:
        relay(*path)
    take_column(nd - 1)
    take_column(0)
    for path in RELAYS[6:]:
        relay(*path)
    nk = 2 * npix
    pick = one_hot(iota((nk, npix), 0) // 2 == iota((nk, npix), 1))
    mg[0:nk, :] = jnp.where(
        lax.rem(iota((nk, rows), 0), 2) == iota((nk, rows), 1) // cols,
        mm(pick, pixp, 1, 1),
        0.0,
    ).astype(BF16)
    tail = mg.shape[0] - nk
    mg[nk:, :] = one_hot(iota((tail, rows), 0) == iota((tail, rows), 1) // cols)
    fetch[3].wait()
    ut[...] = jnp.zeros(ut.shape, BF16)
    ut[heads : 2 * heads, :] = vecs[...]
    spread[...] = one_hot(iota((128, width), 1) // hd == iota((128, width), 0))
    fetch[4].wait()
    fetch[5].wait()
    fetch[6].wait()

    for b in (1, nd - 1, 0):
        arrived(column(1 - core, b), sem_ws.at[b])

    nlate = 2 * nx * 16
    nearly = npd * 16 - nlate
    early = wbuf[0 : nearly // 16].reshape(nearly, cw)
    for cc in range(4):
        sl = slice(cw * cc, cw * (cc + 1))
        t = mm(mts[cc, :, 0:nearly], early)
        b = bias[:, sl].astype(F32)
        vals[0:cols, sl] = t[0:cols] + b[0:1]
        vals[cols:, sl] = t[cols:] + b[1:2]
    take_column(2)
    arrived(column(1 - core, 2), sem_ws.at[2])
    late = wbuf[nearly // 16 :].reshape(nlate, cw)
    for cc in range(4):
        sl = slice(cw * cc, cw * (cc + 1))
        tok[:, sl] = (vals[:, sl] + mm(mts[cc, :, nearly:], late)).astype(BF16)

    zx[...] = mm(tok[...], ut[...], 1, 1)
    for j in range(chunks):
        sl = slice(CHUNK * j, CHUNK * (j + 1))
        vals[:, sl] = mm(tok[...], wv[:, sl])

    for a in range(2):
        for b in range(nz):
            if (a, b) != (0, 0):
                take(a, b)

    def products(j, carry):
        at = pl.multiple_of(j * CHUNK, CHUNK)
        grad = obuf[:, :, pl.ds(at, CHUNK)].astype(F32).reshape(cols, CHUNK)
        prod = vals[:, pl.ds(at, CHUNK)] * jnp.concatenate([grad, grad], axis=0)
        hi = prod.astype(BF16)
        lo = (prod - hi.astype(F32)).astype(BF16)
        part = spread[:, pl.ds(at, CHUNK)]
        zx[...] += mm(hi, part, 1, 1) + mm(lo, part, 1, 1)
        return carry

    lax.fori_loop(0, chunks, products, 0)
    xt = jnp.transpose(zx[...])
    sc, dp = [], []
    for c in range(2):
        s = xt[heads : 2 * heads, cols * c : cols * (c + 1)]
        which = jnp.full(s.shape, slots[2 * v + c], jnp.int32)
        sc.append(jnp.where(which < channels, s, -1e30))
        dp.append(xt[0:heads, cols * c : cols * (c + 1)])

    top = jnp.maximum(sc[0], sc[1])
    e0, e1 = jnp.exp(sc[0] - top), jnp.exp(sc[1] - top)
    total = e0 + e1
    mean = (e0 * dp[0] + e1 * dp[1]) / total
    logsum = top + jnp.log(total)
    for h in range(heads):
        for k, t in enumerate((logsum, mean)):
            st_send[h, 2 * k : 2 * k + 1, :] = t[h : h + 1, 0:128]
            st_send[h, 2 * k + 1 : 2 * k + 2, :] = t[h : h + 1, 128:256]
    spray_v(4, lambda q: st_send.at[q], st_recv)
    st_recv[v] = st_send[v]
    gather_wait(recv, 4, nv, st_recv)
    got = st_recv[...]
    logs = got[:, 0:2, :]
    peak = jnp.max(logs, axis=0)
    scale = jnp.exp(logs - peak[None])
    total = jnp.sum(scale, axis=0)
    res[v, 0:2, :] = peak + jnp.log(total)
    res[v, 2:4, :] = jnp.sum(scale * got[:, 2:4, :], axis=0) / total
    spray_v(5, lambda q: res.at[v], res)
    gather_wait(recv, 5, nv, res)
    for h in range(heads):
        for k in range(2):
            stat[k, h : h + 1, 0:128] = res[h, 2 * k : 2 * k + 1, :]
            stat[k, h : h + 1, 128:256] = res[h, 2 * k + 1 : 2 * k + 2, :]
    logsum, mean = stat[0], stat[1]
    probs = [jnp.exp(s - logsum) for s in sc]
    dscore = jnp.concatenate([a * (b - mean) for a, b in zip(probs, dp)], axis=1)
    probs = jnp.concatenate(probs, axis=1)

    part = mm(dscore.astype(BF16), tok[...])
    nl = width // 128
    for h in range(heads):
        for k in range(nl):
            su_send[h, k : k + 1, :] = part[h : h + 1, 128 * k : 128 * (k + 1)]
    spray_v(6, lambda q: su_send.at[q], su_recv)
    su_recv[v] = su_send[v]

    pad = jnp.zeros((128 - 2 * heads, rows), F32)
    q = jnp.transpose(jnp.concatenate([probs, dscore, pad], axis=0)).astype(BF16)
    grad = obuf[...].reshape(cols, width)
    for j in range(chunks):
        sl = slice(CHUNK * j, CHUNK * (j + 1))
        g = grad[:, sl].astype(F32)
        g = jnp.concatenate([g, g], axis=0)
        act[:, sl] = (mm(q, spread[:, sl]) * g).astype(BF16)
    for j in range(chunks):
        sl = slice(CHUNK * j, CHUNK * (j + 1))
        tg = (mm(act[...], wv[sl, :], 1, 1) + mm(q, ut[:, sl])).astype(BF16)
        g = mm(mg[...], tg)
        for a in range(npa):
            g_send[j, a] = g[16 * a : 16 * (a + 1)]
        for a in range(CHUNK // 128):
            gb_send[j * (CHUNK // 128) + a] = g[nk : nk + 2, 128 * a : 128 * (a + 1)]
        spray(13 + j, npa, p, dev_p, lambda q, j=j: g_send.at[j, q], g_recv.at[j])
    spray(10, npa, p, dev_p, lambda q: gb_send.at[q], gb_recv)

    gather_wait(recv, 6, nv, su_recv)
    su = jnp.sum(su_recv[...], axis=0)
    sp_send[...] = su
    put(sp_send, sp_recv, send.at[7], recv.at[7], sibling)
    arrived(sp_recv, recv.at[7])
    sv_send[...] = su + sp_recv[...]
    spray_chip(8, sv_send, sv_recv)
    sv_recv[chip] = sv_send[...]

    for j in range(chunks):
        g_recv[j, p] = g_send[j, p]
        gather_wait(recv, 13 + j, npa, g_recv.at[j])
        g = jnp.sum(g_recv[j], axis=0)
        for a in range(nd):
            h_send[a, :, CHUNK * j : CHUNK * (j + 1)] = g[4 * a : 4 * (a + 1)]
    spray(11, nd, d, dev_d, lambda q: h_send.at[q], h_recv)
    h_recv[d] = h_send[d]
    gb_recv[p] = gb_send[p]
    gather_wait(recv, 10, npa, gb_recv)
    hb_send[...] = jnp.sum(gb_recv[...], axis=0)
    spray(12, nd, d, dev_d, lambda q: hb_send, hb_recv)
    hb_recv[d] = hb_send[...]

    gather_wait(recv, 8, nchip, sv_recv)
    dub[v] = jnp.sum(sv_recv[...], axis=0)
    spray_v(9, lambda q: dub.at[v], dub)

    gather_wait(recv, 11, nd, h_recv)
    dw = jnp.sum(h_recv[...], axis=0)
    for k in range(2):
        dw_ref[:, width * k : width * (k + 1)] = dw[2 * k : 2 * k + 2]
    gather_wait(recv, 12, nd, hb_recv)
    db = jnp.sum(hb_recv[...], axis=0)
    step = 128 // nd
    out = db[:, 0:step]
    for a in range(1, nd):
        mine = jnp.full(out.shape, d, jnp.int32) == a
        out = jnp.where(mine, db[:, step * a : step * (a + 1)], out)
    db_ref[...] = out

    arrived(wbuf.at[pl.ds(0, len(NEAR_CHIP))], send.at[0])
    gather_wait(send, 1, nv, obuf)
    arrived(wbuf.at[pl.ds(0, nchip)], send.at[2])
    arrived(wbuf.at[pl.ds(0, nx)], send.at[3])
    gather_wait(send, 4, nv, st_recv)
    gather_wait(send, 5, nv, res)
    gather_wait(send, 6, nv, su_recv)
    arrived(sp_recv, send.at[7])
    gather_wait(send, 8, nchip, sv_recv)
    gather_wait(send, 10, npa, gb_recv)
    gather_wait(send, 11, nd, h_recv)
    gather_wait(send, 12, nd, hb_recv)
    for j in range(chunks):
        gather_wait(send, 13 + j, npa, g_recv.at[j])
    gather_wait(recv, 9, nv, dub)
    for h in range(heads):
        for k in range(nl):
            du_ref[h : h + 1, 128 * k : 128 * (k + 1)] = dub[h, k : k + 1, :]
    gather_wait(send, 9, nv, dub)


def store(a_ref, b_ref, c_ref, a_out, b_out, c_out, sem):
    pairs = ((a_ref, a_out), (b_ref, b_out), (c_ref, c_out))
    copies = [
        pltpu.make_async_copy(src, dst, sem.at[i]) for i, (src, dst) in enumerate(pairs)
    ]
    for copy in copies:
        copy.start()
    for copy in copies:
        copy.wait()


def shards(
    sizes, pixels, emb_weight, chan_bias, score_vecs, value_weight, out_grad, slot_order
):
    nv, npa, nd = sizes
    npd = npa * nd
    samples, ch_dev, npix, patches = pixels.shape
    width, heads = score_vecs.shape
    channels = nv * ch_dev - nv // 4
    rows = samples * patches * ch_dev
    per = npix // npd
    pix = pixels.transpose(0, 1, 3, 2).reshape(rows, npix)
    og = out_grad.reshape(samples, width)
    vmem = pl.BlockSpec(memory_space=pltpu.VMEM)
    chunks = width // CHUNK
    dw, db, du = pl.pallas_call(
        functools.partial(kernel, (nv, npa, nd, channels)),
        out_shape=(
            jax.ShapeDtypeStruct((ch_dev, per * width), F32),
            jax.ShapeDtypeStruct((ch_dev, width // npd), F32),
            jax.ShapeDtypeStruct((heads, width), F32),
        ),
        in_specs=[pl.BlockSpec(memory_space=pltpu.HBM)] * 7,
        out_specs=(vmem, vmem, vmem),
        scratch_shapes=[
            pltpu.SMEM(slot_order.shape, jnp.int32),
            pltpu.VMEM((rows, npix), BF16),
            pltpu.VMEM((ch_dev, per * width), BF16),
            pltpu.VMEM((ch_dev, width), BF16),
            pltpu.VMEM((heads, width), BF16),
            pltpu.VMEM((width, width), BF16),
            pltpu.VMEM((4, rows, npd * 16), BF16),
            pltpu.VMEM((npix * ch_dev + 16, rows), BF16),
            pltpu.VMEM((16, width // 4), F32),
            pltpu.VMEM((16, width // 4), BF16),
            pltpu.VMEM((npd, 16, width // 4), BF16),
            pltpu.VMEM((nv, samples, width), BF16),
            pltpu.VMEM((rows, width), BF16),
            pltpu.VMEM((128, width), BF16),
            pltpu.VMEM((128, width), BF16),
            pltpu.VMEM((rows, width), F32),
            pltpu.VMEM((rows, 128), F32),
            pltpu.VMEM((rows, width), BF16),
            pltpu.VMEM((nv, 4, 128), F32),
            pltpu.VMEM((nv, 4, 128), F32),
            pltpu.VMEM((nv, 4, 128), F32),
            pltpu.VMEM((2, heads, rows // 2), F32),
            pltpu.VMEM((nv, width // 128, 128), F32),
            pltpu.VMEM((nv, width // 128, 128), F32),
            pltpu.VMEM((width // 128, 128), F32),
            pltpu.VMEM((width // 128, 128), F32),
            pltpu.VMEM((width // 128, 128), F32),
            pltpu.VMEM((npd // 2, width // 128, 128), F32),
            pltpu.VMEM((nv, width // 128, 128), F32),
            pltpu.VMEM((chunks, npa, 16, CHUNK), F32),
            pltpu.VMEM((chunks, npa, 16, CHUNK), F32),
            pltpu.VMEM((npa, 2, 128), F32),
            pltpu.VMEM((npa, 2, 128), F32),
            pltpu.VMEM((nd, 4, width), F32),
            pltpu.VMEM((nd, 4, width), F32),
            pltpu.VMEM((2, 128), F32),
            pltpu.VMEM((nd, 2, 128), F32),
            pltpu.SemaphoreType.DMA((7,)),
            pltpu.SemaphoreType.DMA((nv,)),
            pltpu.SemaphoreType.DMA((nd,)),
            pltpu.SemaphoreType.DMA((nd,)),
            pltpu.SemaphoreType.DMA((13 + chunks,)),
            pltpu.SemaphoreType.DMA((13 + chunks,)),
        ],
        compiler_params=pltpu.CompilerParams(
            collective_id=0, has_side_effects=True, vmem_limit_bytes=40 * 1024 * 1024
        ),
        name="backward",
    )(*(pltpu.with_memory_space_constraint(x, pltpu.HBM) for x in (slot_order, pix, emb_weight, chan_bias, score_vecs.T, og, value_weight)))
    parts = (dw, db, du)
    hbm = pl.BlockSpec(memory_space=pltpu.HBM)
    dw, db, du = pl.pallas_call(
        store,
        out_shape=tuple(jax.ShapeDtypeStruct(x.shape, F32) for x in parts),
        in_specs=[vmem] * 3,
        out_specs=(hbm,) * 3,
        scratch_shapes=[pltpu.SemaphoreType.DMA((3,))],
        compiler_params=pltpu.CompilerParams(vmem_limit_bytes=4 * 1024 * 1024),
        name="store",
    )(*parts)
    return dw, db, du.T


def solution(mesh):
    sizes = (mesh.shape["var"], mesh.shape["patch"], mesh.shape["dp"])
    in_specs = (
        P("dp", "var", None, "patch"),
        P("var", ("patch", "dp")),
        P("var", None),
        P(),
        P(),
        P("dp", ("patch", "var"), None),
        P(),
    )
    out_specs = (P("var", ("patch", "dp")), P("var", ("patch", "dp")), P())
    return jax.shard_map(
        functools.partial(shards, sizes),
        mesh=mesh,
        in_specs=in_specs,
        out_specs=out_specs,
        check_vma=False,
    )
```

```python
import functools

import jax
import jax.numpy as jnp
from jax import lax
from jax.experimental import pallas as pl
from jax.experimental.pallas import tpu as pltpu
from jax.sharding import PartitionSpec as P

MESH = pl.DeviceIdType.MESH
F32 = jnp.float32
BF16 = jnp.bfloat16
CHUNK = 256
FAR = (4, 3, 5, 2, 6, 1, 7)
NEAR_V = ((1, 2), (1, 6), (0, 2), (0, 6), (1, 1), (1, 7), (0, 1), (0, 7), (1, 0))
NEAR_CHIP = tuple((x, d) for x in (2, 1, 3, 0) for d in (1, 3, 0) if (x, d) != (0, 0))
PLACE = {0: 0, 1: 1, 3: 2, 2: 3}
OWN = ((0, 2), (0, 6), (0, 1), (0, 7), (1, 0))
RELAYS = (
    (0, 6, 0, 2),
    (0, 2, 1, 6),
    (0, 6, 0, 1),
    (0, 2, 0, 7),
    (0, 6, 1, 1),
    (0, 2, 1, 7),
    (1, 0, 0, 1),
    (1, 0, 0, 7),
    (0, 2, 1, 0),
    (0, 6, 1, 0),
)


def mm(a, b, ca=1, cb=0):
    return lax.dot_general(
        a, b, (((ca,), (cb,)), ((), ())), preferred_element_type=F32
    )


def iota(shape, dim):
    return lax.broadcasted_iota(jnp.int32, shape, dim)


def one_hot(cond):
    return jnp.where(cond, 1.0, 0.0).astype(BF16)


def kernel(
    sizes,
    slot_hbm,
    pix_hbm,
    emb_hbm,
    bias_hbm,
    vecs_hbm,
    og_hbm,
    value_hbm,
    dw_ref,
    db_ref,
    du_ref,
    slots,
    pix,
    emb,
    bias,
    vecs,
    wv,
    mts,
    mg,
    wtmp,
    wsend,
    wbuf,
    obuf,
    tok,
    spread,
    ut,
    vals,
    zx,
    act,
    st_send,
    st_recv,
    res,
    stat,
    su_send,
    su_recv,
    sp_send,
    sp_recv,
    sv_send,
    sv_recv,
    dub,
    g_send,
    g_recv,
    gb_send,
    gb_recv,
    h_send,
    h_recv,
    hb_send,
    hb_recv,
    sem_in,
    sem_og,
    sem_w,
    sem_ws,
    send,
    recv,
):
    nv, npa, nd, channels = sizes
    npd = npa * nd
    nchip = npd // 2
    heads = nv
    nz = len(FAR) + 1
    v = lax.axis_index("var")
    p = lax.axis_index("patch")
    d = lax.axis_index("dp")
    core = lax.rem(p, 2)
    x = p // 2
    nx = npa // 2
    chip = d * nx + x
    y, z = v // nz, lax.rem(v, nz)
    width = wv.shape[0]
    hd = width // heads
    rows = mts.shape[1]
    cols = rows // 2
    chunks = width // CHUNK

    fetch = [
        pltpu.make_async_copy(src, dst, sem_in.at[i])
        for i, (src, dst) in enumerate(
            (
                (emb_hbm, emb),
                (og_hbm, obuf.at[v]),
                (pix_hbm, pix),
                (vecs_hbm, vecs),
                (bias_hbm, bias),
                (slot_hbm, slots),
                (value_hbm, wv),
            )
        )
    ]
    def at_v(a, b):
        return lax.rem(y + a, 2) * nz + lax.rem(z + b, nz)

    def at_chip(a, b, c=core):
        return {"patch": lax.rem(x + a, nx) * 2 + c, "dp": lax.rem(d + b, nd)}

    def dev_p(q):
        return {"patch": q}

    def dev_d(q):
        return {"dp": q}

    sibling = dev_p(p + 1 - 2 * core)

    barrier = pltpu.get_barrier_semaphore()
    friends = [at_chip(a, b) for a, b in NEAR_CHIP]
    friends += [{"var": at_v(a, b)} for a, b in NEAR_V] + [sibling]
    friends += [at_chip(0, b, 1 - core) for b in (1, nd - 1)]
    for dev in friends:
        pl.semaphore_signal(barrier, inc=1, device_id=dev, device_id_type=MESH)
    for copy in fetch:
        copy.start()

    def put(src, dst, send_sem, recv_sem, dev):
        pltpu.make_async_remote_copy(
            src_ref=src,
            dst_ref=dst,
            send_sem=send_sem,
            recv_sem=recv_sem,
            device_id=dev,
            device_id_type=MESH,
        ).start()

    def spray(k, count, me, dev, src, dst):
        def one(j, carry):
            q = lax.rem(me + j, count)
            put(src(q), dst.at[me], send.at[k], recv.at[k], dev(q))
            return carry

        lax.fori_loop(1, count, one, 0)

    def spray_v(k, src, dst):
        for a, b in [(a, b) for b in FAR for a in (1, 0)] + [(1, 0)]:
            q = at_v(a, b)
            put(src(q), dst.at[v], send.at[k], recv.at[k], {"var": q})

    def spray_chip(k, src, dst):
        def one(j, carry):
            q = lax.rem(chip + j, nchip)
            to = {"patch": lax.rem(q, nx) * 2 + core, "dp": q // nx}
            put(src, dst.at[chip], send.at[k], recv.at[k], to)
            return carry

        lax.fori_loop(1, nchip, one, 0)

    def arrived(part, sem):
        pltpu.make_async_copy(part, part, sem).wait()

    def gather_wait(sems, k, count, dst):
        arrived(dst.at[pl.ds(0, count - 1)], sems.at[k])

    fetch[0].wait()
    block = emb[...].astype(F32)
    cw = wtmp.shape[1]
    for cc in range(4):
        for k in range(2):
            at = k * width + cc * cw
            wtmp[4 * cc + 2 * k : 4 * cc + 2 * k + 2, :] = block[:, at : at + cw]
    wsend[...] = wtmp[...].astype(BF16)

    pl.semaphore_wait(barrier, len(friends))

    mine = obuf.at[v]
    for a, b in NEAR_CHIP:
        slot = PLACE[-b % nd] * 2 * nx + core * nx + x
        put(wsend, wbuf.at[slot], send.at[0], sem_w.at[-b % nd], at_chip(a, b))
    fetch[1].wait()
    for a, b in OWN:
        put(mine, mine, send.at[1], sem_og.at[v], {"var": at_v(a, b)})
    wbuf[core * nx + x] = wsend[...]

    waited = set()

    def take(a, b):
        u = at_v(a, b)
        if (a, b) not in waited:
            waited.add((a, b))
            arrived(obuf.at[u], sem_og.at[u])
        return u

    def relay(oa, ob, a, b):
        u = take(oa, ob)
        put(obuf.at[u], obuf.at[u], send.at[1], sem_og.at[u], {"var": at_v(a, b)})

    def column(c, b):
        return wbuf.at[pl.ds((PLACE[b] * 2 + c) * nx, nx)]

    def to_sibling(b):
        part = column(core, b)
        put(part, part, send.at[2], sem_ws.at[b], sibling)

    def take_column(b):
        part = column(core, b)
        arrived(part if b else part.at[pl.ds(0, nx - 1)], sem_w.at[b])
        to_sibling(b)

    fetch[2].wait()
    to = iota((rows, rows), 0)
    src = lax.rem(to, 16) * 32 + (to // cols) * 16 + lax.rem(to, cols) // 16
    pixp = mm(one_hot(iota((rows, rows), 1) == src), pix[...]).astype(BF16)
    npix = pixp.shape[1]
    col = iota((npix, rows), 1)
    slot = col // 16
    place = slot // (2 * nx)
    offset = jnp.where(place == 2, 3, jnp.where(place == 3, 2, place))
    owner = 2 * lax.rem(slot, nx) + lax.rem(slot, 2 * nx) // nx
    owner = owner * nd + lax.rem(d + offset, nd)
    of_pix = 2 * owner + lax.rem(col, 4) // 2 == iota((npix, rows), 0)
    same = lax.rem(iota((rows, rows), 1), 2) == to // cols
    for cc in range(4):
        pick = one_hot(of_pix & (lax.rem(col, 16) // 4 == cc))
        mts[cc] = jnp.where(same, mm(pixp, pick), 0.0).astype(BF16)
    def opposite(b, first):
        half = wbuf.at[pl.ds((PLACE[b] * 2 + core) * nx + first, nx // 2)]
        there = wbuf.at[pl.ds((PLACE[2] * 2 + core) * nx + first, nx // 2)]
        for c in (core, 1 - core):
            put(half, there, send.at[3], sem_w.at[2], at_chip(0, nd - b, c))

    take_column(1)
    opposite(1, 0)
    take_column(nd - 1)
    opposite(nd - 1, nx // 2)
    for path in RELAYS[:6]:
        relay(*path)
    take_column(0)
    for path in RELAYS[6:]:
        relay(*path)
    nk = 2 * npix
    pick = one_hot(iota((nk, npix), 0) // 2 == iota((nk, npix), 1))
    mg[0:nk, :] = jnp.where(
        lax.rem(iota((nk, rows), 0), 2) == iota((nk, rows), 1) // cols,
        mm(pick, pixp, 1, 1),
        0.0,
    ).astype(BF16)
    tail = mg.shape[0] - nk
    mg[nk:, :] = one_hot(iota((tail, rows), 0) == iota((tail, rows), 1) // cols)
    fetch[3].wait()
    ut[...] = jnp.zeros(ut.shape, BF16)
    ut[heads : 2 * heads, :] = vecs[...]
    spread[...] = one_hot(iota((128, width), 1) // hd == iota((128, width), 0))
    fetch[4].wait()
    fetch[5].wait()
    fetch[6].wait()

    for b in (1, nd - 1, 0):
        arrived(column(1 - core, b), sem_ws.at[b])

    nlate = 2 * nx * 16
    nearly = npd * 16 - nlate
    early = wbuf[0 : nearly // 16].reshape(nearly, cw)
    for cc in range(4):
        sl = slice(cw * cc, cw * (cc + 1))
        t = mm(mts[cc, :, 0:nearly], early)
        b = bias[:, sl].astype(F32)
        vals[0:cols, sl] = t[0:cols] + b[0:1]
        vals[cols:, sl] = t[cols:] + b[1:2]
    arrived(wbuf.at[pl.ds(nearly // 16, 2 * nx)], sem_w.at[2])
    late = wbuf[nearly // 16 :].reshape(nlate, cw)
    for cc in range(4):
        sl = slice(cw * cc, cw * (cc + 1))
        tok[:, sl] = (vals[:, sl] + mm(mts[cc, :, nearly:], late)).astype(BF16)

    zx[...] = mm(tok[...], ut[...], 1, 1)
    for j in range(chunks):
        sl = slice(CHUNK * j, CHUNK * (j + 1))
        vals[:, sl] = mm(tok[...], wv[:, sl])

    for a in range(2):
        for b in range(nz):
            if (a, b) != (0, 0):
                take(a, b)

    def products(j, carry):
        at = pl.multiple_of(j * CHUNK, CHUNK)
        grad = obuf[:, :, pl.ds(at, CHUNK)].astype(F32).reshape(cols, CHUNK)
        prod = vals[:, pl.ds(at, CHUNK)] * jnp.concatenate([grad, grad], axis=0)
        hi = prod.astype(BF16)
        lo = (prod - hi.astype(F32)).astype(BF16)
        part = spread[:, pl.ds(at, CHUNK)]
        zx[...] += mm(hi, part, 1, 1) + mm(lo, part, 1, 1)
        return carry

    lax.fori_loop(0, chunks, products, 0)
    xt = jnp.transpose(zx[...])
    sc, dp = [], []
    for c in range(2):
        s = xt[heads : 2 * heads, cols * c : cols * (c + 1)]
        which = jnp.full(s.shape, slots[2 * v + c], jnp.int32)
        sc.append(jnp.where(which < channels, s, -1e30))
        dp.append(xt[0:heads, cols * c : cols * (c + 1)])

    top = jnp.maximum(sc[0], sc[1])
    e0, e1 = jnp.exp(sc[0] - top), jnp.exp(sc[1] - top)
    total = e0 + e1
    mean = (e0 * dp[0] + e1 * dp[1]) / total
    logsum = top + jnp.log(total)
    for h in range(heads):
        for k, t in enumerate((logsum, mean)):
            st_send[h, 2 * k : 2 * k + 1, :] = t[h : h + 1, 0:128]
            st_send[h, 2 * k + 1 : 2 * k + 2, :] = t[h : h + 1, 128:256]
    spray_v(4, lambda q: st_send.at[q], st_recv)
    st_recv[v] = st_send[v]
    gather_wait(recv, 4, nv, st_recv)
    got = st_recv[...]
    logs = got[:, 0:2, :]
    peak = jnp.max(logs, axis=0)
    scale = jnp.exp(logs - peak[None])
    total = jnp.sum(scale, axis=0)
    res[v, 0:2, :] = peak + jnp.log(total)
    res[v, 2:4, :] = jnp.sum(scale * got[:, 2:4, :], axis=0) / total
    spray_v(5, lambda q: res.at[v], res)
    gather_wait(recv, 5, nv, res)
    for h in range(heads):
        for k in range(2):
            stat[k, h : h + 1, 0:128] = res[h, 2 * k : 2 * k + 1, :]
            stat[k, h : h + 1, 128:256] = res[h, 2 * k + 1 : 2 * k + 2, :]
    logsum, mean = stat[0], stat[1]
    probs = [jnp.exp(s - logsum) for s in sc]
    dscore = jnp.concatenate([a * (b - mean) for a, b in zip(probs, dp)], axis=1)
    probs = jnp.concatenate(probs, axis=1)

    part = mm(dscore.astype(BF16), tok[...])
    nl = width // 128
    for h in range(heads):
        for k in range(nl):
            su_send[h, k : k + 1, :] = part[h : h + 1, 128 * k : 128 * (k + 1)]
    spray_v(6, lambda q: su_send.at[q], su_recv)
    su_recv[v] = su_send[v]

    pad = jnp.zeros((128 - 2 * heads, rows), F32)
    q = jnp.transpose(jnp.concatenate([probs, dscore, pad], axis=0)).astype(BF16)
    grad = obuf[...].reshape(cols, width)
    for j in range(chunks):
        sl = slice(CHUNK * j, CHUNK * (j + 1))
        g = grad[:, sl].astype(F32)
        g = jnp.concatenate([g, g], axis=0)
        act[:, sl] = (mm(q, spread[:, sl]) * g).astype(BF16)
    for j in range(chunks):
        sl = slice(CHUNK * j, CHUNK * (j + 1))
        tg = (mm(act[...], wv[sl, :], 1, 1) + mm(q, ut[:, sl])).astype(BF16)
        g = mm(mg[...], tg)
        for a in range(npa):
            g_send[j, a] = g[16 * a : 16 * (a + 1)]
        for a in range(CHUNK // 128):
            gb_send[j * (CHUNK // 128) + a] = g[nk : nk + 2, 128 * a : 128 * (a + 1)]
        spray(13 + j, npa, p, dev_p, lambda q, j=j: g_send.at[j, q], g_recv.at[j])
    spray(10, npa, p, dev_p, lambda q: gb_send.at[q], gb_recv)

    gather_wait(recv, 6, nv, su_recv)
    su = jnp.sum(su_recv[...], axis=0)
    sp_send[...] = su
    put(sp_send, sp_recv, send.at[7], recv.at[7], sibling)
    arrived(sp_recv, recv.at[7])
    sv_send[...] = su + sp_recv[...]
    spray_chip(8, sv_send, sv_recv)
    sv_recv[chip] = sv_send[...]

    for j in range(chunks):
        g_recv[j, p] = g_send[j, p]
        gather_wait(recv, 13 + j, npa, g_recv.at[j])
        g = jnp.sum(g_recv[j], axis=0)
        for a in range(nd):
            h_send[a, :, CHUNK * j : CHUNK * (j + 1)] = g[4 * a : 4 * (a + 1)]
    spray(11, nd, d, dev_d, lambda q: h_send.at[q], h_recv)
    h_recv[d] = h_send[d]
    gb_recv[p] = gb_send[p]
    gather_wait(recv, 10, npa, gb_recv)
    hb_send[...] = jnp.sum(gb_recv[...], axis=0)
    spray(12, nd, d, dev_d, lambda q: hb_send, hb_recv)
    hb_recv[d] = hb_send[...]

    gather_wait(recv, 8, nchip, sv_recv)
    dub[v] = jnp.sum(sv_recv[...], axis=0)
    spray_v(9, lambda q: dub.at[v], dub)

    gather_wait(recv, 11, nd, h_recv)
    dw = jnp.sum(h_recv[...], axis=0)
    for k in range(2):
        dw_ref[:, width * k : width * (k + 1)] = dw[2 * k : 2 * k + 2]
    gather_wait(recv, 12, nd, hb_recv)
    db = jnp.sum(hb_recv[...], axis=0)
    step = 128 // nd
    out = db[:, 0:step]
    for a in range(1, nd):
        mine = jnp.full(out.shape, d, jnp.int32) == a
        out = jnp.where(mine, db[:, step * a : step * (a + 1)], out)
    db_ref[...] = out

    arrived(wbuf.at[pl.ds(0, len(NEAR_CHIP))], send.at[0])
    gather_wait(send, 1, nv, obuf)
    arrived(wbuf.at[pl.ds(0, 3 * nx)], send.at[2])
    arrived(wbuf.at[pl.ds(0, 2 * nx)], send.at[3])
    gather_wait(send, 4, nv, st_recv)
    gather_wait(send, 5, nv, res)
    gather_wait(send, 6, nv, su_recv)
    arrived(sp_recv, send.at[7])
    gather_wait(send, 8, nchip, sv_recv)
    gather_wait(send, 10, npa, gb_recv)
    gather_wait(send, 11, nd, h_recv)
    gather_wait(send, 12, nd, hb_recv)
    for j in range(chunks):
        gather_wait(send, 13 + j, npa, g_recv.at[j])
    gather_wait(recv, 9, nv, dub)
    for h in range(heads):
        for k in range(nl):
            du_ref[h : h + 1, 128 * k : 128 * (k + 1)] = dub[h, k : k + 1, :]
    gather_wait(send, 9, nv, dub)


def store(a_ref, b_ref, c_ref, a_out, b_out, c_out, sem):
    pairs = ((a_ref, a_out), (b_ref, b_out), (c_ref, c_out))
    copies = [
        pltpu.make_async_copy(src, dst, sem.at[i]) for i, (src, dst) in enumerate(pairs)
    ]
    for copy in copies:
        copy.start()
    for copy in copies:
        copy.wait()


def shards(
    sizes, pixels, emb_weight, chan_bias, score_vecs, value_weight, out_grad, slot_order
):
    nv, npa, nd = sizes
    npd = npa * nd
    samples, ch_dev, npix, patches = pixels.shape
    width, heads = score_vecs.shape
    channels = nv * ch_dev - nv // 4
    rows = samples * patches * ch_dev
    per = npix // npd
    pix = pixels.transpose(0, 1, 3, 2).reshape(rows, npix)
    og = out_grad.reshape(samples, width)
    vmem = pl.BlockSpec(memory_space=pltpu.VMEM)
    chunks = width // CHUNK
    dw, db, du = pl.pallas_call(
        functools.partial(kernel, (nv, npa, nd, channels)),
        out_shape=(
            jax.ShapeDtypeStruct((ch_dev, per * width), F32),
            jax.ShapeDtypeStruct((ch_dev, width // npd), F32),
            jax.ShapeDtypeStruct((heads, width), F32),
        ),
        in_specs=[pl.BlockSpec(memory_space=pltpu.HBM)] * 7,
        out_specs=(vmem, vmem, vmem),
        scratch_shapes=[
            pltpu.SMEM(slot_order.shape, jnp.int32),
            pltpu.VMEM((rows, npix), BF16),
            pltpu.VMEM((ch_dev, per * width), BF16),
            pltpu.VMEM((ch_dev, width), BF16),
            pltpu.VMEM((heads, width), BF16),
            pltpu.VMEM((width, width), BF16),
            pltpu.VMEM((4, rows, npd * 16), BF16),
            pltpu.VMEM((npix * ch_dev + 16, rows), BF16),
            pltpu.VMEM((16, width // 4), F32),
            pltpu.VMEM((16, width // 4), BF16),
            pltpu.VMEM((npd, 16, width // 4), BF16),
            pltpu.VMEM((nv, samples, width), BF16),
            pltpu.VMEM((rows, width), BF16),
            pltpu.VMEM((128, width), BF16),
            pltpu.VMEM((128, width), BF16),
            pltpu.VMEM((rows, width), F32),
            pltpu.VMEM((rows, 128), F32),
            pltpu.VMEM((rows, width), BF16),
            pltpu.VMEM((nv, 4, 128), F32),
            pltpu.VMEM((nv, 4, 128), F32),
            pltpu.VMEM((nv, 4, 128), F32),
            pltpu.VMEM((2, heads, rows // 2), F32),
            pltpu.VMEM((nv, width // 128, 128), F32),
            pltpu.VMEM((nv, width // 128, 128), F32),
            pltpu.VMEM((width // 128, 128), F32),
            pltpu.VMEM((width // 128, 128), F32),
            pltpu.VMEM((width // 128, 128), F32),
            pltpu.VMEM((npd // 2, width // 128, 128), F32),
            pltpu.VMEM((nv, width // 128, 128), F32),
            pltpu.VMEM((chunks, npa, 16, CHUNK), F32),
            pltpu.VMEM((chunks, npa, 16, CHUNK), F32),
            pltpu.VMEM((npa, 2, 128), F32),
            pltpu.VMEM((npa, 2, 128), F32),
            pltpu.VMEM((nd, 4, width), F32),
            pltpu.VMEM((nd, 4, width), F32),
            pltpu.VMEM((2, 128), F32),
            pltpu.VMEM((nd, 2, 128), F32),
            pltpu.SemaphoreType.DMA((7,)),
            pltpu.SemaphoreType.DMA((nv,)),
            pltpu.SemaphoreType.DMA((nd,)),
            pltpu.SemaphoreType.DMA((nd,)),
            pltpu.SemaphoreType.DMA((13 + chunks,)),
            pltpu.SemaphoreType.DMA((13 + chunks,)),
        ],
        compiler_params=pltpu.CompilerParams(
            collective_id=0, has_side_effects=True, vmem_limit_bytes=40 * 1024 * 1024
        ),
        name="backward",
    )(*(pltpu.with_memory_space_constraint(x, pltpu.HBM) for x in (slot_order, pix, emb_weight, chan_bias, score_vecs.T, og, value_weight)))
    parts = (dw, db, du)
    hbm = pl.BlockSpec(memory_space=pltpu.HBM)
    dw, db, du = pl.pallas_call(
        store,
        out_shape=tuple(jax.ShapeDtypeStruct(x.shape, F32) for x in parts),
        in_specs=[vmem] * 3,
        out_specs=(hbm,) * 3,
        scratch_shapes=[pltpu.SemaphoreType.DMA((3,))],
        compiler_params=pltpu.CompilerParams(vmem_limit_bytes=4 * 1024 * 1024),
        name="store",
    )(*parts)
    return dw, db, du.T


def solution(mesh):
    sizes = (mesh.shape["var"], mesh.shape["patch"], mesh.shape["dp"])
    in_specs = (
        P("dp", "var", None, "patch"),
        P("var", ("patch", "dp")),
        P("var", None),
        P(),
        P(),
        P("dp", ("patch", "var"), None),
        P(),
    )
    out_specs = (P("var", ("patch", "dp")), P("var", ("patch", "dp")), P())
    return jax.shard_map(
        functools.partial(shards, sizes),
        mesh=mesh,
        in_specs=in_specs,
        out_specs=out_specs,
        check_vma=False,
    )
```

```python
import functools

import jax
import jax.numpy as jnp
from jax import lax
from jax.experimental import pallas as pl
from jax.experimental.pallas import tpu as pltpu
from jax.sharding import PartitionSpec as P

MESH = pl.DeviceIdType.MESH
F32 = jnp.float32
BF16 = jnp.bfloat16
CHUNK = 256
FAR = (4, 3, 5, 2, 6, 1, 7)
NEAR_V = ((1, 2), (1, 6), (0, 2), (0, 6), (1, 1), (1, 7), (0, 1), (0, 7), (1, 0))
NEAR_CHIP = ((0, 2), (0, 1), (0, 3), (2, 0), (1, 0), (3, 0))
PLACE = {0: 0, 1: 1, 3: 2, 2: 3}
OWN = ((0, 2), (0, 6), (0, 1), (0, 7), (1, 0))
RELAYS = (
    (0, 6, 0, 2),
    (0, 2, 1, 6),
    (0, 6, 0, 1),
    (0, 2, 0, 7),
    (0, 6, 1, 1),
    (0, 2, 1, 7),
    (1, 0, 0, 1),
    (1, 0, 0, 7),
    (0, 2, 1, 0),
    (0, 6, 1, 0),
)


def mm(a, b, ca=1, cb=0):
    return lax.dot_general(
        a, b, (((ca,), (cb,)), ((), ())), preferred_element_type=F32
    )


def iota(shape, dim):
    return lax.broadcasted_iota(jnp.int32, shape, dim)


def one_hot(cond):
    return jnp.where(cond, 1.0, 0.0).astype(BF16)


def kernel(
    sizes,
    slot_hbm,
    pix_hbm,
    emb_hbm,
    bias_hbm,
    vecs_hbm,
    og_hbm,
    value_hbm,
    dw_ref,
    db_ref,
    du_ref,
    slots,
    pix,
    emb,
    bias,
    vecs,
    wv,
    mts,
    mg,
    wtmp,
    wsend,
    wbuf,
    obuf,
    tok,
    spread,
    ut,
    vals,
    zx,
    act,
    st_send,
    st_recv,
    res,
    stat,
    su_send,
    su_recv,
    sp_send,
    sp_recv,
    sv_send,
    sv_recv,
    dub,
    g_send,
    g_recv,
    gb_send,
    gb_recv,
    h_send,
    h_recv,
    hb_send,
    hb_recv,
    sem_in,
    sem_og,
    sem_w,
    sem_ws,
    send,
    recv,
):
    nv, npa, nd, channels = sizes
    npd = npa * nd
    nchip = npd // 2
    heads = nv
    nz = len(FAR) + 1
    v = lax.axis_index("var")
    p = lax.axis_index("patch")
    d = lax.axis_index("dp")
    core = lax.rem(p, 2)
    x = p // 2
    nx = npa // 2
    chip = d * nx + x
    y, z = v // nz, lax.rem(v, nz)
    width = wv.shape[0]
    hd = width // heads
    rows = mts.shape[1]
    cols = rows // 2
    chunks = width // CHUNK

    fetch = [
        pltpu.make_async_copy(src, dst, sem_in.at[i])
        for i, (src, dst) in enumerate(
            (
                (emb_hbm, emb),
                (og_hbm, obuf.at[v]),
                (pix_hbm, pix),
                (vecs_hbm, vecs),
                (bias_hbm, bias),
                (slot_hbm, slots),
                (value_hbm, wv),
            )
        )
    ]
    def at_v(a, b):
        return lax.rem(y + a, 2) * nz + lax.rem(z + b, nz)

    def at_chip(a, b):
        return {"patch": lax.rem(x + a, nx) * 2 + core, "dp": lax.rem(d + b, nd)}

    def dev_p(q):
        return {"patch": q}

    def dev_d(q):
        return {"dp": q}

    sibling = dev_p(p + 1 - 2 * core)

    barrier = pltpu.get_barrier_semaphore()
    friends = [at_chip(a, b) for a, b in NEAR_CHIP]
    friends += [{"var": at_v(a, b)} for a, b in NEAR_V] + [sibling]
    for dev in friends:
        pl.semaphore_signal(barrier, inc=1, device_id=dev, device_id_type=MESH)
    for copy in fetch:
        copy.start()

    def put(src, dst, send_sem, recv_sem, dev):
        pltpu.make_async_remote_copy(
            src_ref=src,
            dst_ref=dst,
            send_sem=send_sem,
            recv_sem=recv_sem,
            device_id=dev,
            device_id_type=MESH,
        ).start()

    def spray(k, count, me, dev, src, dst):
        def one(j, carry):
            q = lax.rem(me + j, count)
            put(src(q), dst.at[me], send.at[k], recv.at[k], dev(q))
            return carry

        lax.fori_loop(1, count, one, 0)

    def spray_v(k, src, dst):
        for a, b in [(a, b) for b in FAR for a in (1, 0)] + [(1, 0)]:
            q = at_v(a, b)
            put(src(q), dst.at[v], send.at[k], recv.at[k], {"var": q})

    def spray_chip(k, src, dst):
        def one(j, carry):
            q = lax.rem(chip + j, nchip)
            to = {"patch": lax.rem(q, nx) * 2 + core, "dp": q // nx}
            put(src, dst.at[chip], send.at[k], recv.at[k], to)
            return carry

        lax.fori_loop(1, nchip, one, 0)

    def arrived(part, sem):
        pltpu.make_async_copy(part, part, sem).wait()

    def gather_wait(sems, k, count, dst):
        arrived(dst.at[pl.ds(0, count - 1)], sems.at[k])

    fetch[0].wait()
    block = emb[...].astype(F32)
    cw = wtmp.shape[1]
    for cc in range(4):
        for k in range(2):
            at = k * width + cc * cw
            wtmp[4 * cc + 2 * k : 4 * cc + 2 * k + 2, :] = block[:, at : at + cw]
    wsend[...] = wtmp[...].astype(BF16)

    pl.semaphore_wait(barrier, len(friends))

    mine = obuf.at[v]
    for a in (2, 1, 3):
        put(wsend, wbuf.at[core * nx + x], send.at[0], sem_w.at[0], at_chip(a, 0))
    fetch[1].wait()
    for a, b in OWN:
        put(mine, mine, send.at[1], sem_og.at[v], {"var": at_v(a, b)})
    wbuf[core * nx + x] = wsend[...]

    waited = set()

    def take(a, b):
        u = at_v(a, b)
        if (a, b) not in waited:
            waited.add((a, b))
            arrived(obuf.at[u], sem_og.at[u])
        return u

    def relay(oa, ob, a, b):
        u = take(oa, ob)
        put(obuf.at[u], obuf.at[u], send.at[1], sem_og.at[u], {"var": at_v(a, b)})

    def column(c, b):
        return wbuf.at[pl.ds((PLACE[b] * 2 + c) * nx, nx)]

    def to_sibling(b):
        part = column(core, b)
        put(part, part, send.at[2], sem_ws.at[b], sibling)

    def take_column(b):
        part = column(core, b)
        arrived(part if b else part.at[pl.ds(0, nx - 1)], sem_w.at[b])
        to_sibling(b)

    fetch[2].wait()
    to = iota((rows, rows), 0)
    src = lax.rem(to, 16) * 32 + (to // cols) * 16 + lax.rem(to, cols) // 16
    pixp = mm(one_hot(iota((rows, rows), 1) == src), pix[...]).astype(BF16)
    npix = pixp.shape[1]
    col = iota((npix, rows), 1)
    slot = col // 16
    place = slot // (2 * nx)
    offset = jnp.where(place == 2, 3, jnp.where(place == 3, 2, place))
    owner = 2 * lax.rem(slot, nx) + lax.rem(slot, 2 * nx) // nx
    owner = owner * nd + lax.rem(d + offset, nd)
    of_pix = 2 * owner + lax.rem(col, 4) // 2 == iota((npix, rows), 0)
    same = lax.rem(iota((rows, rows), 1), 2) == to // cols
    take_column(0)
    for b in (2, 1, nd - 1):
        to = column(core, -b % nd)
        put(column(core, 0), to, send.at[3], sem_w.at[-b % nd], at_chip(0, b))
    for cc in range(4):
        pick = one_hot(of_pix & (lax.rem(col, 16) // 4 == cc))
        mts[cc] = jnp.where(same, mm(pixp, pick), 0.0).astype(BF16)
    for path in RELAYS[:6]:
        relay(*path)
    take_column(1)
    take_column(nd - 1)
    for path in RELAYS[6:]:
        relay(*path)
    nk = 2 * npix
    pick = one_hot(iota((nk, npix), 0) // 2 == iota((nk, npix), 1))
    mg[0:nk, :] = jnp.where(
        lax.rem(iota((nk, rows), 0), 2) == iota((nk, rows), 1) // cols,
        mm(pick, pixp, 1, 1),
        0.0,
    ).astype(BF16)
    tail = mg.shape[0] - nk
    mg[nk:, :] = one_hot(iota((tail, rows), 0) == iota((tail, rows), 1) // cols)
    fetch[3].wait()
    ut[...] = jnp.zeros(ut.shape, BF16)
    ut[heads : 2 * heads, :] = vecs[...]
    spread[...] = one_hot(iota((128, width), 1) // hd == iota((128, width), 0))
    fetch[4].wait()
    fetch[5].wait()
    fetch[6].wait()

    for b in (1, nd - 1, 0):
        arrived(column(1 - core, b), sem_ws.at[b])

    nlate = 2 * nx * 16
    nearly = npd * 16 - nlate
    early = wbuf[0 : nearly // 16].reshape(nearly, cw)
    for cc in range(4):
        sl = slice(cw * cc, cw * (cc + 1))
        t = mm(mts[cc, :, 0:nearly], early)
        b = bias[:, sl].astype(F32)
        vals[0:cols, sl] = t[0:cols] + b[0:1]
        vals[cols:, sl] = t[cols:] + b[1:2]
    take_column(2)
    arrived(column(1 - core, 2), sem_ws.at[2])
    late = wbuf[nearly // 16 :].reshape(nlate, cw)
    for cc in range(4):
        sl = slice(cw * cc, cw * (cc + 1))
        tok[:, sl] = (vals[:, sl] + mm(mts[cc, :, nearly:], late)).astype(BF16)

    zx[...] = mm(tok[...], ut[...], 1, 1)
    for j in range(chunks):
        sl = slice(CHUNK * j, CHUNK * (j + 1))
        vals[:, sl] = mm(tok[...], wv[:, sl])

    for a in range(2):
        for b in range(nz):
            if (a, b) != (0, 0):
                take(a, b)

    def products(j, carry):
        at = pl.multiple_of(j * CHUNK, CHUNK)
        grad = obuf[:, :, pl.ds(at, CHUNK)].astype(F32).reshape(cols, CHUNK)
        prod = vals[:, pl.ds(at, CHUNK)] * jnp.concatenate([grad, grad], axis=0)
        hi = prod.astype(BF16)
        lo = (prod - hi.astype(F32)).astype(BF16)
        part = spread[:, pl.ds(at, CHUNK)]
        zx[...] += mm(hi, part, 1, 1) + mm(lo, part, 1, 1)
        return carry

    lax.fori_loop(0, chunks, products, 0)
    xt = jnp.transpose(zx[...])
    sc, dp = [], []
    for c in range(2):
        s = xt[heads : 2 * heads, cols * c : cols * (c + 1)]
        which = jnp.full(s.shape, slots[2 * v + c], jnp.int32)
        sc.append(jnp.where(which < channels, s, -1e30))
        dp.append(xt[0:heads, cols * c : cols * (c + 1)])

    top = jnp.maximum(sc[0], sc[1])
    e0, e1 = jnp.exp(sc[0] - top), jnp.exp(sc[1] - top)
    total = e0 + e1
    mean = (e0 * dp[0] + e1 * dp[1]) / total
    logsum = top + jnp.log(total)
    for h in range(heads):
        for k, t in enumerate((logsum, mean)):
            st_send[h, 2 * k : 2 * k + 1, :] = t[h : h + 1, 0:128]
            st_send[h, 2 * k + 1 : 2 * k + 2, :] = t[h : h + 1, 128:256]
    spray_v(4, lambda q: st_send.at[q], st_recv)
    st_recv[v] = st_send[v]
    gather_wait(recv, 4, nv, st_recv)
    got = st_recv[...]
    logs = got[:, 0:2, :]
    peak = jnp.max(logs, axis=0)
    scale = jnp.exp(logs - peak[None])
    total = jnp.sum(scale, axis=0)
    res[v, 0:2, :] = peak + jnp.log(total)
    res[v, 2:4, :] = jnp.sum(scale * got[:, 2:4, :], axis=0) / total
    spray_v(5, lambda q: res.at[v], res)
    gather_wait(recv, 5, nv, res)
    for h in range(heads):
        for k in range(2):
            stat[k, h : h + 1, 0:128] = res[h, 2 * k : 2 * k + 1, :]
            stat[k, h : h + 1, 128:256] = res[h, 2 * k + 1 : 2 * k + 2, :]
    logsum, mean = stat[0], stat[1]
    probs = [jnp.exp(s - logsum) for s in sc]
    dscore = jnp.concatenate([a * (b - mean) for a, b in zip(probs, dp)], axis=1)
    probs = jnp.concatenate(probs, axis=1)

    part = mm(dscore.astype(BF16), tok[...])
    nl = width // 128
    for h in range(heads):
        for k in range(nl):
            su_send[h, k : k + 1, :] = part[h : h + 1, 128 * k : 128 * (k + 1)]
    spray_v(6, lambda q: su_send.at[q], su_recv)
    su_recv[v] = su_send[v]

    pad = jnp.zeros((128 - 2 * heads, rows), F32)
    q = jnp.transpose(jnp.concatenate([probs, dscore, pad], axis=0)).astype(BF16)
    grad = obuf[...].reshape(cols, width)
    for j in range(chunks):
        sl = slice(CHUNK * j, CHUNK * (j + 1))
        g = grad[:, sl].astype(F32)
        g = jnp.concatenate([g, g], axis=0)
        act[:, sl] = (mm(q, spread[:, sl]) * g).astype(BF16)
    for j in range(chunks):
        sl = slice(CHUNK * j, CHUNK * (j + 1))
        tg = (mm(act[...], wv[sl, :], 1, 1) + mm(q, ut[:, sl])).astype(BF16)
        g = mm(mg[...], tg)
        for a in range(npa):
            g_send[j, a] = g[16 * a : 16 * (a + 1)]
        for a in range(CHUNK // 128):
            gb_send[j * (CHUNK // 128) + a] = g[nk : nk + 2, 128 * a : 128 * (a + 1)]
        spray(13 + j, npa, p, dev_p, lambda q, j=j: g_send.at[j, q], g_recv.at[j])
    spray(10, npa, p, dev_p, lambda q: gb_send.at[q], gb_recv)

    gather_wait(recv, 6, nv, su_recv)
    su = jnp.sum(su_recv[...], axis=0)
    sp_send[...] = su
    put(sp_send, sp_recv, send.at[7], recv.at[7], sibling)
    arrived(sp_recv, recv.at[7])
    sv_send[...] = su + sp_recv[...]
    spray_chip(8, sv_send, sv_recv)
    sv_recv[chip] = sv_send[...]

    for j in range(chunks):
        g_recv[j, p] = g_send[j, p]
        gather_wait(recv, 13 + j, npa, g_recv.at[j])
        g = jnp.sum(g_recv[j], axis=0)
        for a in range(nd):
            h_send[a, :, CHUNK * j : CHUNK * (j + 1)] = g[4 * a : 4 * (a + 1)]
    spray(11, nd, d, dev_d, lambda q: h_send.at[q], h_recv)
    h_recv[d] = h_send[d]
    gb_recv[p] = gb_send[p]
    gather_wait(recv, 10, npa, gb_recv)
    hb_send[...] = jnp.sum(gb_recv[...], axis=0)
    spray(12, nd, d, dev_d, lambda q: hb_send, hb_recv)
    hb_recv[d] = hb_send[...]

    gather_wait(recv, 8, nchip, sv_recv)
    dub[v] = jnp.sum(sv_recv[...], axis=0)
    spray_v(9, lambda q: dub.at[v], dub)

    gather_wait(recv, 11, nd, h_recv)
    dw = jnp.sum(h_recv[...], axis=0)
    for k in range(2):
        dw_ref[:, width * k : width * (k + 1)] = dw[2 * k : 2 * k + 2]
    gather_wait(recv, 12, nd, hb_recv)
    db = jnp.sum(hb_recv[...], axis=0)
    step = 128 // nd
    out = db[:, 0:step]
    for a in range(1, nd):
        mine = jnp.full(out.shape, d, jnp.int32) == a
        out = jnp.where(mine, db[:, step * a : step * (a + 1)], out)
    db_ref[...] = out

    arrived(wbuf.at[pl.ds(0, nx - 1)], send.at[0])
    gather_wait(send, 1, nv, obuf)
    arrived(wbuf.at[pl.ds(0, nchip)], send.at[2])
    arrived(wbuf.at[pl.ds(0, 3 * nx)], send.at[3])
    gather_wait(send, 4, nv, st_recv)
    gather_wait(send, 5, nv, res)
    gather_wait(send, 6, nv, su_recv)
    arrived(sp_recv, send.at[7])
    gather_wait(send, 8, nchip, sv_recv)
    gather_wait(send, 10, npa, gb_recv)
    gather_wait(send, 11, nd, h_recv)
    gather_wait(send, 12, nd, hb_recv)
    for j in range(chunks):
        gather_wait(send, 13 + j, npa, g_recv.at[j])
    gather_wait(recv, 9, nv, dub)
    for h in range(heads):
        for k in range(nl):
            du_ref[h : h + 1, 128 * k : 128 * (k + 1)] = dub[h, k : k + 1, :]
    gather_wait(send, 9, nv, dub)


def store(a_ref, b_ref, c_ref, a_out, b_out, c_out, sem):
    pairs = ((a_ref, a_out), (b_ref, b_out), (c_ref, c_out))
    copies = [
        pltpu.make_async_copy(src, dst, sem.at[i]) for i, (src, dst) in enumerate(pairs)
    ]
    for copy in copies:
        copy.start()
    for copy in copies:
        copy.wait()


def shards(
    sizes, pixels, emb_weight, chan_bias, score_vecs, value_weight, out_grad, slot_order
):
    nv, npa, nd = sizes
    npd = npa * nd
    samples, ch_dev, npix, patches = pixels.shape
    width, heads = score_vecs.shape
    channels = nv * ch_dev - nv // 4
    rows = samples * patches * ch_dev
    per = npix // npd
    pix = pixels.transpose(0, 1, 3, 2).reshape(rows, npix)
    og = out_grad.reshape(samples, width)
    vmem = pl.BlockSpec(memory_space=pltpu.VMEM)
    chunks = width // CHUNK
    dw, db, du = pl.pallas_call(
        functools.partial(kernel, (nv, npa, nd, channels)),
        out_shape=(
            jax.ShapeDtypeStruct((ch_dev, per * width), F32),
            jax.ShapeDtypeStruct((ch_dev, width // npd), F32),
            jax.ShapeDtypeStruct((heads, width), F32),
        ),
        in_specs=[pl.BlockSpec(memory_space=pltpu.HBM)] * 7,
        out_specs=(vmem, vmem, vmem),
        scratch_shapes=[
            pltpu.SMEM(slot_order.shape, jnp.int32),
            pltpu.VMEM((rows, npix), BF16),
            pltpu.VMEM((ch_dev, per * width), BF16),
            pltpu.VMEM((ch_dev, width), BF16),
            pltpu.VMEM((heads, width), BF16),
            pltpu.VMEM((width, width), BF16),
            pltpu.VMEM((4, rows, npd * 16), BF16),
            pltpu.VMEM((npix * ch_dev + 16, rows), BF16),
            pltpu.VMEM((16, width // 4), F32),
            pltpu.VMEM((16, width // 4), BF16),
            pltpu.VMEM((npd, 16, width // 4), BF16),
            pltpu.VMEM((nv, samples, width), BF16),
            pltpu.VMEM((rows, width), BF16),
            pltpu.VMEM((128, width), BF16),
            pltpu.VMEM((128, width), BF16),
            pltpu.VMEM((rows, width), F32),
            pltpu.VMEM((rows, 128), F32),
            pltpu.VMEM((rows, width), BF16),
            pltpu.VMEM((nv, 4, 128), F32),
            pltpu.VMEM((nv, 4, 128), F32),
            pltpu.VMEM((nv, 4, 128), F32),
            pltpu.VMEM((2, heads, rows // 2), F32),
            pltpu.VMEM((nv, width // 128, 128), F32),
            pltpu.VMEM((nv, width // 128, 128), F32),
            pltpu.VMEM((width // 128, 128), F32),
            pltpu.VMEM((width // 128, 128), F32),
            pltpu.VMEM((width // 128, 128), F32),
            pltpu.VMEM((npd // 2, width // 128, 128), F32),
            pltpu.VMEM((nv, width // 128, 128), F32),
            pltpu.VMEM((chunks, npa, 16, CHUNK), F32),
            pltpu.VMEM((chunks, npa, 16, CHUNK), F32),
            pltpu.VMEM((npa, 2, 128), F32),
            pltpu.VMEM((npa, 2, 128), F32),
            pltpu.VMEM((nd, 4, width), F32),
            pltpu.VMEM((nd, 4, width), F32),
            pltpu.VMEM((2, 128), F32),
            pltpu.VMEM((nd, 2, 128), F32),
            pltpu.SemaphoreType.DMA((7,)),
            pltpu.SemaphoreType.DMA((nv,)),
            pltpu.SemaphoreType.DMA((nd,)),
            pltpu.SemaphoreType.DMA((nd,)),
            pltpu.SemaphoreType.DMA((13 + chunks,)),
            pltpu.SemaphoreType.DMA((13 + chunks,)),
        ],
        compiler_params=pltpu.CompilerParams(
            collective_id=0, has_side_effects=True, vmem_limit_bytes=40 * 1024 * 1024
        ),
        name="backward",
    )(*(pltpu.with_memory_space_constraint(x, pltpu.HBM) for x in (slot_order, pix, emb_weight, chan_bias, score_vecs.T, og, value_weight)))
    parts = (dw, db, du)
    hbm = pl.BlockSpec(memory_space=pltpu.HBM)
    dw, db, du = pl.pallas_call(
        store,
        out_shape=tuple(jax.ShapeDtypeStruct(x.shape, F32) for x in parts),
        in_specs=[vmem] * 3,
        out_specs=(hbm,) * 3,
        scratch_shapes=[pltpu.SemaphoreType.DMA((3,))],
        compiler_params=pltpu.CompilerParams(vmem_limit_bytes=4 * 1024 * 1024),
        name="store",
    )(*parts)
    return dw, db, du.T


def solution(mesh):
    sizes = (mesh.shape["var"], mesh.shape["patch"], mesh.shape["dp"])
    in_specs = (
        P("dp", "var", None, "patch"),
        P("var", ("patch", "dp")),
        P("var", None),
        P(),
        P(),
        P("dp", ("patch", "var"), None),
        P(),
    )
    out_specs = (P("var", ("patch", "dp")), P("var", ("patch", "dp")), P())
    return jax.shard_map(
        functools.partial(shards, sizes),
        mesh=mesh,
        in_specs=in_specs,
        out_specs=out_specs,
        check_vma=False,
    )
```

```python
import functools

import jax
import jax.numpy as jnp
from jax import lax
from jax.experimental import pallas as pl
from jax.experimental.pallas import tpu as pltpu
from jax.sharding import PartitionSpec as P

MESH = pl.DeviceIdType.MESH
F32 = jnp.float32
BF16 = jnp.bfloat16
CHUNK = 512
FAR = (4, 3, 5, 2, 6, 1, 7)
NEAR_V = ((1, 2), (1, 6), (0, 2), (0, 6), (1, 1), (1, 7), (0, 1), (0, 7), (1, 0))
NEAR_CHIP = tuple((x, d) for x in (2, 1, 3, 0) for d in (1, 3, 0) if (x, d) != (0, 0))
PLACE = {0: 0, 1: 1, 3: 2, 2: 3}
OWN = ((0, 2), (0, 6), (0, 1), (0, 7), (1, 0))
RELAYS = (
    (0, 6, 0, 2),
    (0, 2, 1, 6),
    (0, 6, 0, 1),
    (0, 2, 0, 7),
    (0, 6, 1, 1),
    (0, 2, 1, 7),
    (1, 0, 0, 1),
    (1, 0, 0, 7),
    (0, 2, 1, 0),
    (0, 6, 1, 0),
)


def mm(a, b, ca=1, cb=0):
    return lax.dot_general(
        a, b, (((ca,), (cb,)), ((), ())), preferred_element_type=F32
    )


def iota(shape, dim):
    return lax.broadcasted_iota(jnp.int32, shape, dim)


def one_hot(cond):
    return jnp.where(cond, 1.0, 0.0).astype(BF16)


def kernel(
    sizes,
    slot_hbm,
    pix_hbm,
    emb_hbm,
    bias_hbm,
    vecs_hbm,
    og_hbm,
    value_hbm,
    dw_ref,
    db_ref,
    du_ref,
    slots,
    pix,
    emb,
    bias,
    vecs,
    wv,
    mts,
    mg,
    wtmp,
    wsend,
    wbuf,
    obuf,
    tok,
    spread,
    ut,
    vals,
    zx,
    act,
    st_send,
    st_recv,
    res,
    stat,
    su_send,
    su_recv,
    sp_send,
    sp_recv,
    sv_send,
    sv_recv,
    dub,
    g_send,
    g_recv,
    gb_send,
    gb_recv,
    h_send,
    h_recv,
    hb_send,
    hb_recv,
    sem_in,
    sem_og,
    sem_w,
    sem_ws,
    send,
    recv,
):
    nv, npa, nd, channels = sizes
    npd = npa * nd
    nchip = npd // 2
    heads = nv
    nz = len(FAR) + 1
    v = lax.axis_index("var")
    p = lax.axis_index("patch")
    d = lax.axis_index("dp")
    core = lax.rem(p, 2)
    x = p // 2
    nx = npa // 2
    chip = d * nx + x
    y, z = v // nz, lax.rem(v, nz)
    width = wv.shape[0]
    hd = width // heads
    rows = mts.shape[1]
    cols = rows // 2
    chunks = width // CHUNK

    fetch = [
        pltpu.make_async_copy(src, dst, sem_in.at[i])
        for i, (src, dst) in enumerate(
            (
                (emb_hbm, emb),
                (og_hbm, obuf.at[v]),
                (pix_hbm, pix),
                (vecs_hbm, vecs),
                (bias_hbm, bias),
                (slot_hbm, slots),
                (value_hbm, wv),
            )
        )
    ]
    def at_v(a, b):
        return lax.rem(y + a, 2) * nz + lax.rem(z + b, nz)

    def at_chip(a, b):
        return {"patch": lax.rem(x + a, nx) * 2 + core, "dp": lax.rem(d + b, nd)}

    def dev_p(q):
        return {"patch": q}

    def dev_d(q):
        return {"dp": q}

    sibling = dev_p(p + 1 - 2 * core)

    barrier = pltpu.get_barrier_semaphore()
    friends = [at_chip(a, b) for a, b in NEAR_CHIP]
    friends += [{"var": at_v(a, b)} for a, b in NEAR_V] + [sibling]
    for dev in friends:
        pl.semaphore_signal(barrier, inc=1, device_id=dev, device_id_type=MESH)
    for copy in fetch:
        copy.start()

    def put(src, dst, send_sem, recv_sem, dev):
        pltpu.make_async_remote_copy(
            src_ref=src,
            dst_ref=dst,
            send_sem=send_sem,
            recv_sem=recv_sem,
            device_id=dev,
            device_id_type=MESH,
        ).start()

    def spray(k, count, me, dev, src, dst):
        def one(j, carry):
            q = lax.rem(me + j, count)
            put(src(q), dst.at[me], send.at[k], recv.at[k], dev(q))
            return carry

        lax.fori_loop(1, count, one, 0)

    def spray_v(k, src, dst):
        for a, b in [(a, b) for b in FAR for a in (1, 0)] + [(1, 0)]:
            q = at_v(a, b)
            put(src(q), dst.at[v], send.at[k], recv.at[k], {"var": q})

    def spray_chip(k, src, dst):
        def one(j, carry):
            q = lax.rem(chip + j, nchip)
            to = {"patch": lax.rem(q, nx) * 2 + core, "dp": q // nx}
            put(src, dst.at[chip], send.at[k], recv.at[k], to)
            return carry

        lax.fori_loop(1, nchip, one, 0)

    def arrived(part, sem):
        pltpu.make_async_copy(part, part, sem).wait()

    def gather_wait(sems, k, count, dst):
        arrived(dst.at[pl.ds(0, count - 1)], sems.at[k])

    fetch[0].wait()
    block = emb[...].astype(F32)
    cw = wtmp.shape[1]
    for cc in range(4):
        for k in range(2):
            at = k * width + cc * cw
            wtmp[4 * cc + 2 * k : 4 * cc + 2 * k + 2, :] = block[:, at : at + cw]
    wsend[...] = wtmp[...].astype(BF16)

    pl.semaphore_wait(barrier, len(friends))

    mine = obuf.at[v]
    for a, b in NEAR_CHIP:
        slot = PLACE[-b % nd] * 2 * nx + core * nx + x
        put(wsend, wbuf.at[slot], send.at[0], sem_w.at[-b % nd], at_chip(a, b))
    fetch[1].wait()
    for a, b in OWN:
        put(mine, mine, send.at[1], sem_og.at[v], {"var": at_v(a, b)})
    wbuf[core * nx + x] = wsend[...]

    waited = set()

    def take(a, b):
        u = at_v(a, b)
        if (a, b) not in waited:
            waited.add((a, b))
            arrived(obuf.at[u], sem_og.at[u])
        return u

    def relay(oa, ob, a, b):
        u = take(oa, ob)
        put(obuf.at[u], obuf.at[u], send.at[1], sem_og.at[u], {"var": at_v(a, b)})

    def column(c, b):
        return wbuf.at[pl.ds((PLACE[b] * 2 + c) * nx, nx)]

    def to_sibling(b):
        part = column(core, b)
        put(part, part, send.at[2], sem_ws.at[b], sibling)

    def take_column(b):
        part = column(core, b)
        arrived(part if b else part.at[pl.ds(0, nx - 1)], sem_w.at[b])
        to_sibling(b)

    fetch[2].wait()
    to = iota((rows, rows), 0)
    src = lax.rem(to, 16) * 32 + (to // cols) * 16 + lax.rem(to, cols) // 16
    pixp = mm(one_hot(iota((rows, rows), 1) == src), pix[...]).astype(BF16)
    npix = pixp.shape[1]
    col = iota((npix, rows), 1)
    slot = col // 16
    place = slot // (2 * nx)
    offset = jnp.where(place == 2, 3, jnp.where(place == 3, 2, place))
    owner = 2 * lax.rem(slot, nx) + lax.rem(slot, 2 * nx) // nx
    owner = owner * nd + lax.rem(d + offset, nd)
    of_pix = 2 * owner + lax.rem(col, 4) // 2 == iota((npix, rows), 0)
    same = lax.rem(iota((rows, rows), 1), 2) == to // cols
    for cc in range(4):
        pick = one_hot(of_pix & (lax.rem(col, 16) // 4 == cc))
        mts[cc] = jnp.where(same, mm(pixp, pick), 0.0).astype(BF16)
    take_column(1)
    put(column(core, 1), column(core, 2), send.at[3], sem_w.at[2], at_chip(0, nd - 1))
    for path in RELAYS[:6]:
        relay(*path)
    take_column(nd - 1)
    take_column(0)
    for path in RELAYS[6:]:
        relay(*path)
    nk = 2 * npix
    pick = one_hot(iota((nk, npix), 0) // 2 == iota((nk, npix), 1))
    mg[0:nk, :] = jnp.where(
        lax.rem(iota((nk, rows), 0), 2) == iota((nk, rows), 1) // cols,
        mm(pick, pixp, 1, 1),
        0.0,
    ).astype(BF16)
    tail = mg.shape[0] - nk
    mg[nk:, :] = one_hot(iota((tail, rows), 0) == iota((tail, rows), 1) // cols)
    fetch[3].wait()
    ut[...] = jnp.zeros(ut.shape, BF16)
    ut[heads : 2 * heads, :] = vecs[...]
    spread[...] = one_hot(iota((128, width), 1) // hd == iota((128, width), 0))
    fetch[4].wait()
    fetch[5].wait()
    fetch[6].wait()

    for b in (1, nd - 1, 0):
        arrived(column(1 - core, b), sem_ws.at[b])

    nlate = 2 * nx * 16
    nearly = npd * 16 - nlate
    early = wbuf[0 : nearly // 16].reshape(nearly, cw)
    for cc in range(4):
        sl = slice(cw * cc, cw * (cc + 1))
        t = mm(mts[cc, :, 0:nearly], early)
        b = bias[:, sl].astype(F32)
        vals[0:cols, sl] = t[0:cols] + b[0:1]
        vals[cols:, sl] = t[cols:] + b[1:2]
    take_column(2)
    arrived(column(1 - core, 2), sem_ws.at[2])
    late = wbuf[nearly // 16 :].reshape(nlate, cw)
    for cc in range(4):
        sl = slice(cw * cc, cw * (cc + 1))
        tok[:, sl] = (vals[:, sl] + mm(mts[cc, :, nearly:], late)).astype(BF16)

    zx[...] = mm(tok[...], ut[...], 1, 1)
    for j in range(chunks):
        sl = slice(CHUNK * j, CHUNK * (j + 1))
        vals[:, sl] = mm(tok[...], wv[:, sl])

    for a in range(2):
        for b in range(nz):
            if (a, b) != (0, 0):
                take(a, b)

    def products(j, carry):
        at = pl.multiple_of(j * CHUNK, CHUNK)
        grad = obuf[:, :, pl.ds(at, CHUNK)].astype(F32).reshape(cols, CHUNK)
        prod = vals[:, pl.ds(at, CHUNK)] * jnp.concatenate([grad, grad], axis=0)
        hi = prod.astype(BF16)
        lo = (prod - hi.astype(F32)).astype(BF16)
        part = spread[:, pl.ds(at, CHUNK)]
        zx[...] += mm(hi, part, 1, 1) + mm(lo, part, 1, 1)
        return carry

    lax.fori_loop(0, chunks, products, 0)
    xt = jnp.transpose(zx[...])
    sc, dp = [], []
    for c in range(2):
        s = xt[heads : 2 * heads, cols * c : cols * (c + 1)]
        which = jnp.full(s.shape, slots[2 * v + c], jnp.int32)
        sc.append(jnp.where(which < channels, s, -1e30))
        dp.append(xt[0:heads, cols * c : cols * (c + 1)])

    top = jnp.maximum(sc[0], sc[1])
    e0, e1 = jnp.exp(sc[0] - top), jnp.exp(sc[1] - top)
    total = e0 + e1
    mean = (e0 * dp[0] + e1 * dp[1]) / total
    logsum = top + jnp.log(total)
    for h in range(heads):
        for k, t in enumerate((logsum, mean)):
            st_send[h, 2 * k : 2 * k + 1, :] = t[h : h + 1, 0:128]
            st_send[h, 2 * k + 1 : 2 * k + 2, :] = t[h : h + 1, 128:256]
    spray_v(4, lambda q: st_send.at[q], st_recv)
    st_recv[v] = st_send[v]
    gather_wait(recv, 4, nv, st_recv)
    got = st_recv[...]
    logs = got[:, 0:2, :]
    peak = jnp.max(logs, axis=0)
    scale = jnp.exp(logs - peak[None])
    total = jnp.sum(scale, axis=0)
    res[v, 0:2, :] = peak + jnp.log(total)
    res[v, 2:4, :] = jnp.sum(scale * got[:, 2:4, :], axis=0) / total
    spray_v(5, lambda q: res.at[v], res)
    gather_wait(recv, 5, nv, res)
    for h in range(heads):
        for k in range(2):
            stat[k, h : h + 1, 0:128] = res[h, 2 * k : 2 * k + 1, :]
            stat[k, h : h + 1, 128:256] = res[h, 2 * k + 1 : 2 * k + 2, :]
    logsum, mean = stat[0], stat[1]
    probs = [jnp.exp(s - logsum) for s in sc]
    dscore = jnp.concatenate([a * (b - mean) for a, b in zip(probs, dp)], axis=1)
    probs = jnp.concatenate(probs, axis=1)

    part = mm(dscore.astype(BF16), tok[...])
    nl = width // 128
    for h in range(heads):
        for k in range(nl):
            su_send[h, k : k + 1, :] = part[h : h + 1, 128 * k : 128 * (k + 1)]
    spray_v(6, lambda q: su_send.at[q], su_recv)
    su_recv[v] = su_send[v]

    pad = jnp.zeros((128 - 2 * heads, rows), F32)
    q = jnp.transpose(jnp.concatenate([probs, dscore, pad], axis=0)).astype(BF16)
    grad = obuf[...].reshape(cols, width)
    for j in range(chunks):
        sl = slice(CHUNK * j, CHUNK * (j + 1))
        g = grad[:, sl].astype(F32)
        g = jnp.concatenate([g, g], axis=0)
        act[:, sl] = (mm(q, spread[:, sl]) * g).astype(BF16)
    for j in range(chunks):
        sl = slice(CHUNK * j, CHUNK * (j + 1))
        tg = (mm(act[...], wv[sl, :], 1, 1) + mm(q, ut[:, sl])).astype(BF16)
        g = mm(mg[...], tg)
        for a in range(npa):
            g_send[j, a] = g[16 * a : 16 * (a + 1)]
        for a in range(CHUNK // 128):
            gb_send[j * (CHUNK // 128) + a] = g[nk : nk + 2, 128 * a : 128 * (a + 1)]
        spray(13 + j, npa, p, dev_p, lambda q, j=j: g_send.at[j, q], g_recv.at[j])
    spray(10, npa, p, dev_p, lambda q: gb_send.at[q], gb_recv)

    gather_wait(recv, 6, nv, su_recv)
    su = jnp.sum(su_recv[...], axis=0)
    sp_send[...] = su
    put(sp_send, sp_recv, send.at[7], recv.at[7], sibling)
    arrived(sp_recv, recv.at[7])
    sv_send[...] = su + sp_recv[...]
    spray_chip(8, sv_send, sv_recv)
    sv_recv[chip] = sv_send[...]

    for j in range(chunks):
        g_recv[j, p] = g_send[j, p]
        gather_wait(recv, 13 + j, npa, g_recv.at[j])
        g = jnp.sum(g_recv[j], axis=0)
        for a in range(nd):
            h_send[a, :, CHUNK * j : CHUNK * (j + 1)] = g[4 * a : 4 * (a + 1)]
    spray(11, nd, d, dev_d, lambda q: h_send.at[q], h_recv)
    h_recv[d] = h_send[d]
    gb_recv[p] = gb_send[p]
    gather_wait(recv, 10, npa, gb_recv)
    hb_send[...] = jnp.sum(gb_recv[...], axis=0)
    spray(12, nd, d, dev_d, lambda q: hb_send, hb_recv)
    hb_recv[d] = hb_send[...]

    gather_wait(recv, 8, nchip, sv_recv)
    dub[v] = jnp.sum(sv_recv[...], axis=0)
    spray_v(9, lambda q: dub.at[v], dub)

    gather_wait(recv, 11, nd, h_recv)
    dw = jnp.sum(h_recv[...], axis=0)
    for k in range(2):
        dw_ref[:, width * k : width * (k + 1)] = dw[2 * k : 2 * k + 2]
    gather_wait(recv, 12, nd, hb_recv)
    db = jnp.sum(hb_recv[...], axis=0)
    step = 128 // nd
    out = db[:, 0:step]
    for a in range(1, nd):
        mine = jnp.full(out.shape, d, jnp.int32) == a
        out = jnp.where(mine, db[:, step * a : step * (a + 1)], out)
    db_ref[...] = out

    arrived(wbuf.at[pl.ds(0, len(NEAR_CHIP))], send.at[0])
    gather_wait(send, 1, nv, obuf)
    arrived(wbuf.at[pl.ds(0, nchip)], send.at[2])
    arrived(wbuf.at[pl.ds(0, nx)], send.at[3])
    gather_wait(send, 4, nv, st_recv)
    gather_wait(send, 5, nv, res)
    gather_wait(send, 6, nv, su_recv)
    arrived(sp_recv, send.at[7])
    gather_wait(send, 8, nchip, sv_recv)
    gather_wait(send, 10, npa, gb_recv)
    gather_wait(send, 11, nd, h_recv)
    gather_wait(send, 12, nd, hb_recv)
    for j in range(chunks):
        gather_wait(send, 13 + j, npa, g_recv.at[j])
    gather_wait(recv, 9, nv, dub)
    for h in range(heads):
        for k in range(nl):
            du_ref[h : h + 1, 128 * k : 128 * (k + 1)] = dub[h, k : k + 1, :]
    gather_wait(send, 9, nv, dub)


def store(a_ref, b_ref, c_ref, a_out, b_out, c_out, sem):
    pairs = ((a_ref, a_out), (b_ref, b_out), (c_ref, c_out))
    copies = [
        pltpu.make_async_copy(src, dst, sem.at[i]) for i, (src, dst) in enumerate(pairs)
    ]
    for copy in copies:
        copy.start()
    for copy in copies:
        copy.wait()


def shards(
    sizes, pixels, emb_weight, chan_bias, score_vecs, value_weight, out_grad, slot_order
):
    nv, npa, nd = sizes
    npd = npa * nd
    samples, ch_dev, npix, patches = pixels.shape
    width, heads = score_vecs.shape
    channels = nv * ch_dev - nv // 4
    rows = samples * patches * ch_dev
    per = npix // npd
    pix = pixels.transpose(0, 1, 3, 2).reshape(rows, npix)
    og = out_grad.reshape(samples, width)
    vmem = pl.BlockSpec(memory_space=pltpu.VMEM)
    chunks = width // CHUNK
    dw, db, du = pl.pallas_call(
        functools.partial(kernel, (nv, npa, nd, channels)),
        out_shape=(
            jax.ShapeDtypeStruct((ch_dev, per * width), F32),
            jax.ShapeDtypeStruct((ch_dev, width // npd), F32),
            jax.ShapeDtypeStruct((heads, width), F32),
        ),
        in_specs=[pl.BlockSpec(memory_space=pltpu.HBM)] * 7,
        out_specs=(vmem, vmem, vmem),
        scratch_shapes=[
            pltpu.SMEM(slot_order.shape, jnp.int32),
            pltpu.VMEM((rows, npix), BF16),
            pltpu.VMEM((ch_dev, per * width), BF16),
            pltpu.VMEM((ch_dev, width), BF16),
            pltpu.VMEM((heads, width), BF16),
            pltpu.VMEM((width, width), BF16),
            pltpu.VMEM((4, rows, npd * 16), BF16),
            pltpu.VMEM((npix * ch_dev + 16, rows), BF16),
            pltpu.VMEM((16, width // 4), F32),
            pltpu.VMEM((16, width // 4), BF16),
            pltpu.VMEM((npd, 16, width // 4), BF16),
            pltpu.VMEM((nv, samples, width), BF16),
            pltpu.VMEM((rows, width), BF16),
            pltpu.VMEM((128, width), BF16),
            pltpu.VMEM((128, width), BF16),
            pltpu.VMEM((rows, width), F32),
            pltpu.VMEM((rows, 128), F32),
            pltpu.VMEM((rows, width), BF16),
            pltpu.VMEM((nv, 4, 128), F32),
            pltpu.VMEM((nv, 4, 128), F32),
            pltpu.VMEM((nv, 4, 128), F32),
            pltpu.VMEM((2, heads, rows // 2), F32),
            pltpu.VMEM((nv, width // 128, 128), F32),
            pltpu.VMEM((nv, width // 128, 128), F32),
            pltpu.VMEM((width // 128, 128), F32),
            pltpu.VMEM((width // 128, 128), F32),
            pltpu.VMEM((width // 128, 128), F32),
            pltpu.VMEM((npd // 2, width // 128, 128), F32),
            pltpu.VMEM((nv, width // 128, 128), F32),
            pltpu.VMEM((chunks, npa, 16, CHUNK), F32),
            pltpu.VMEM((chunks, npa, 16, CHUNK), F32),
            pltpu.VMEM((npa, 2, 128), F32),
            pltpu.VMEM((npa, 2, 128), F32),
            pltpu.VMEM((nd, 4, width), F32),
            pltpu.VMEM((nd, 4, width), F32),
            pltpu.VMEM((2, 128), F32),
            pltpu.VMEM((nd, 2, 128), F32),
            pltpu.SemaphoreType.DMA((7,)),
            pltpu.SemaphoreType.DMA((nv,)),
            pltpu.SemaphoreType.DMA((nd,)),
            pltpu.SemaphoreType.DMA((nd,)),
            pltpu.SemaphoreType.DMA((13 + chunks,)),
            pltpu.SemaphoreType.DMA((13 + chunks,)),
        ],
        compiler_params=pltpu.CompilerParams(
            collective_id=0, has_side_effects=True, vmem_limit_bytes=40 * 1024 * 1024
        ),
        name="backward",
    )(*(pltpu.with_memory_space_constraint(x, pltpu.HBM) for x in (slot_order, pix, emb_weight, chan_bias, score_vecs.T, og, value_weight)))
    parts = (dw, db, du)
    hbm = pl.BlockSpec(memory_space=pltpu.HBM)
    dw, db, du = pl.pallas_call(
        store,
        out_shape=tuple(jax.ShapeDtypeStruct(x.shape, F32) for x in parts),
        in_specs=[vmem] * 3,
        out_specs=(hbm,) * 3,
        scratch_shapes=[pltpu.SemaphoreType.DMA((3,))],
        compiler_params=pltpu.CompilerParams(vmem_limit_bytes=4 * 1024 * 1024),
        name="store",
    )(*parts)
    return dw, db, du.T


def solution(mesh):
    sizes = (mesh.shape["var"], mesh.shape["patch"], mesh.shape["dp"])
    in_specs = (
        P("dp", "var", None, "patch"),
        P("var", ("patch", "dp")),
        P("var", None),
        P(),
        P(),
        P("dp", ("patch", "var"), None),
        P(),
    )
    out_specs = (P("var", ("patch", "dp")), P("var", ("patch", "dp")), P())
    return jax.shard_map(
        functools.partial(shards, sizes),
        mesh=mesh,
        in_specs=in_specs,
        out_specs=out_specs,
        check_vma=False,
    )
```
